32 devices in a mesh: row: 4 (over y, x), col: 8 (over z, core).
Axes of the slice: x: 2, y: 2, z: 4, core: 2. Of those that a mesh axis runs over, the one named last changes fastest.
Arguments:
- q_seq: bfloat16 [512, 6144], P('row', 'col'), may hold values from -4.5 to 4.5
- k_seq: bfloat16 [512, 6144], P('row', 'col'), may hold values from -4.5 to 4.5
- v_seq: bfloat16 [512, 6144], P('row', 'col'), may hold values from -6 to 6
- resid: bfloat16 [512, 6144], P('row', 'col'), may hold values from -90 to 90
- ln_gain: float32 [6144], replicated, may hold values from 0.1 to 1.9
- w_up: bfloat16 [6144, 24576], P('row', 'col'), may hold values from -0.078125 to 0.078125
Outputs:
- hidden: bfloat16 [512, 24576], P('row', 'col')
The draws below stay inside these ranges and needn't reach their ends.
All inputs are finite; a program needn't handle non-finite values.
Results may differ from the reference program's by a relative error of at most 0.0051.
Values may be sent and summed in bfloat16 or wider, within the bound.
A program may use at most 128 MiB of HBM per device.

```python
import math
import jax
import jax.numpy as jnp
from jax import lax

HD = 128
FF = 24576
SEQ = 128
D = 6144
TOKENS = 512
N_ROW = 4


def draw_q_seq(key, part):
    values = jnp.clip(jax.random.normal(jax.random.fold_in(key, 1), (TOKENS, D), jnp.float32), -4.5, 4.5)
    return values.astype(jnp.bfloat16)


def draw_k_seq(key, part):
    values = jnp.clip(jax.random.normal(jax.random.fold_in(key, 2), (TOKENS, D), jnp.float32), -4.5, 4.5)
    return values.astype(jnp.bfloat16)


def draw_resid(key, part):
    first = jax.random.fold_in(key, 11)
    second = jax.random.fold_in(key, 12)
    third = jax.random.fold_in(key, 13)
    column = jnp.arange(D).astype(jnp.float32) / D
    base = jnp.clip(jax.random.normal(first, (TOKENS, D), jnp.float32), -4.0, 4.0)
    scales = jnp.exp(jnp.log(0.3) + jnp.log(10.0) * column)
    scales = scales * jax.random.uniform(second, (D,), jnp.float32, 0.7, 1.4)
    row_scale = 0.5 * jnp.exp(jax.random.uniform(third, (TOKENS, 1), jnp.float32) * jnp.log(10.0))
    return (base * scales[None, :] * row_scale).astype(jnp.bfloat16)


def block_scale(own_key, extent, split, least, high):
    level = 1.0
    for dim, blocks in split:
        draws = jax.random.uniform(jax.random.fold_in(jax.random.fold_in(own_key, 6), dim), (blocks,), jnp.float32, least / len(split), high / len(split))
        level = level * jnp.repeat(jnp.exp(draws), extent[dim] // blocks).reshape((-1,) + (1,) * (len(extent) - 1 - dim))
    return level


def scatter_about(rng, shape, scale, most, shards=(), kind=jnp.bfloat16):
    factor_of = block_scale(rng, shape, shards, -0.22, 0.18) if shards else 1.0
    entries = jax.random.normal(rng, shape, jnp.float32) * scale * factor_of
    return jnp.minimum(jnp.maximum(entries, -most), most).astype(kind)


def setup_inputs(seed: int = 0) -> dict:
    seeds = jax.random.split(jax.random.key(seed), 7)
    q_seq = draw_q_seq(jax.random.fold_in(seeds[6], 71), 0)
    k_seq = draw_k_seq(jax.random.fold_in(seeds[6], 71), 0)
    v_seq = scatter_about(seeds[2], (TOKENS, D), 1.0, 6.0, ((0, 4), (1, 8)))
    resid = draw_resid(jax.random.fold_in(seeds[6], 71), 0)
    ln_gain = jnp.clip(1.0 + 0.18 * jax.random.normal(seeds[4], (D,), jnp.float32), 0.1, 1.9)
    w_up = scatter_about(seeds[5], (D, FF), D ** -0.5, 0.078125, ((0, 4), (1, 8)))
    return dict(q_seq=q_seq, k_seq=k_seq, v_seq=v_seq, resid=resid, ln_gain=ln_gain, w_up=w_up)


def attention_block(query, keys, values):
    seq, width = query.shape
    heads = width // HD
    qfloat = query.reshape(seq, heads, HD).astype(jnp.float32)
    kfloat = keys.reshape(seq, heads, HD).astype(jnp.float32)
    vfloat = values.reshape(seq, heads, HD).astype(jnp.float32)
    scores = jnp.einsum('qhd,khd->hqk', qfloat, kfloat) * (1.0 / math.sqrt(HD))
    rows_idx = lax.broadcasted_iota(jnp.int32, (seq, seq), 0)
    cols_idx = lax.broadcasted_iota(jnp.int32, (seq, seq), 1)
    scores = jnp.where((rows_idx >= cols_idx)[None], scores, -1e+30)
    highest = lax.optimization_barrier(jnp.max(scores, axis=-1, keepdims=True))
    expo = jnp.exp(scores - highest)
    prob = (expo / lax.optimization_barrier(jnp.sum(expo, axis=-1, keepdims=True))).astype(jnp.bfloat16)
    output = jnp.einsum('hqk,khd->qhd', prob.astype(jnp.float32), vfloat)
    return output.astype(jnp.bfloat16).reshape(seq, width)

def normalize(stream, gain):
    width = stream.shape[1]
    mean = lax.optimization_barrier(jnp.sum(stream, axis=1, keepdims=True)) / width
    spread = lax.optimization_barrier(jnp.sum(stream * stream, axis=1, keepdims=True)) / width - mean * mean
    return ((stream - mean) * lax.rsqrt(spread + 1e-05) * gain[None, :]).astype(jnp.bfloat16)

def reference(q_seq, k_seq, v_seq, resid, ln_gain, w_up):
    shaped = (N_ROW, SEQ, D)

    def attend_blocks(blocks):
        return attention_block(blocks[0], blocks[1], blocks[2])
    attended = lax.map(attend_blocks, (q_seq.reshape(shaped), k_seq.reshape(shaped), v_seq.reshape(shaped)))

    def layer_rows(blocks):
        stream = blocks[0].astype(jnp.float32) + blocks[1].astype(jnp.float32)
        normed = normalize(stream, ln_gain)
        product = jnp.dot(normed, w_up, preferred_element_type=jnp.float32)
        return jax.nn.gelu(product, approximate=True).astype(jnp.bfloat16)
    hidden = lax.map(layer_rows, (resid.reshape(shaped), attended))
    return hidden.reshape(TOKENS, FF)
```

```python
import functools
import math

import jax
import jax.numpy as jnp
from jax import lax
from jax.experimental import pallas as pl
from jax.experimental.pallas import tpu as pltpu
from jax.sharding import PartitionSpec as P

HD = 128
CORES = 2
CHUNKS = 4
TILE = 512
MESH = pl.DeviceIdType.MESH


def guarded(cond, fn):
    if cond is True:
        fn()
    else:
        pl.when(cond)(fn)


def kernel(
    nrow, ncol,
    q_ref, k_ref, v_ref, resid_ref, gain_ref, w_hbm, out_ref,
    w_ref, stream, stats, zbuf, xbuf, pbuf, rbuf, own, acc_ref,
    w_sem, st_s, st_r, z_s, z_r, p_s, p_r, b_s, b_r, r_s, r_r,
):
    seq, width = q_ref.shape
    cols = out_ref.shape[1]
    ratio = ncol // nrow
    nz = ncol // CORES
    ct = seq // CHUNKS
    full = width * ncol
    row, col = lax.axis_index("row"), lax.axis_index("col")
    z, core = lax.div(col, CORES), lax.rem(col, CORES)
    sibling = z * CORES + 1 - core
    sends = []

    def remote(src, dst, send_sem, recv_sem, dev):
        return pltpu.make_async_remote_copy(
            src_ref=src, dst_ref=dst, send_sem=send_sem, recv_sem=recv_sem,
            device_id=dev, device_id_type=MESH,
        )

    w_copy = pltpu.make_async_copy(w_hbm, w_ref, w_sem)
    w_copy.start()

    barrier = pltpu.get_barrier_semaphore()
    for d in range(1, ncol):
        pl.semaphore_signal(barrier, inc=1, device_id=(row, lax.rem(col + d, ncol)), device_id_type=MESH)
    for d in range(1, nrow):
        pl.semaphore_signal(barrier, inc=1, device_id=(lax.rem(row + d, nrow), col), device_id_type=MESH)

    causal = lax.broadcasted_iota(jnp.int32, (seq, seq), 0) >= lax.broadcasted_iota(jnp.int32, (seq, seq), 1)
    s1 = jnp.zeros((seq, 1), jnp.float32)
    s2 = jnp.zeros((seq, 1), jnp.float32)
    for h in range(width // HD):
        cut = slice(h * HD, (h + 1) * HD)
        scores = lax.dot_general(
            q_ref[:, cut], k_ref[:, cut], (((1,), (1,)), ((), ())), preferred_element_type=jnp.float32
        ) * (1.0 / math.sqrt(HD))
        scores = jnp.where(causal, scores, -1e30)
        expo = jnp.exp(scores - jnp.max(scores, axis=-1, keepdims=True))
        prob = (expo / jnp.sum(expo, axis=-1, keepdims=True)).astype(jnp.bfloat16)
        attended = jnp.dot(prob, v_ref[:, cut], preferred_element_type=jnp.float32).astype(jnp.bfloat16)
        part = resid_ref[:, cut].astype(jnp.float32) + attended.astype(jnp.float32)
        stream[:, cut] = part
        s1 += jnp.sum(part, axis=1, keepdims=True)
        s2 += jnp.sum(part * part, axis=1, keepdims=True)

    lane = lax.broadcasted_iota(jnp.int32, (seq, HD), 1)
    packed = jnp.where(lane == 0, s1, jnp.where(lane == 1, s2, 0.0))
    stats[col] = packed.T[:8]
    pl.semaphore_wait(barrier, ncol + nrow - 2)
    for d in range(1, ncol):
        copy = remote(stats.at[col], stats.at[col], st_s.at[d - 1], st_r.at[col], (row, lax.rem(col + d, ncol)))
        copy.start()
        sends.append((True, copy))
    for d in range(1, ncol):
        other = lax.rem(col + d, ncol)
        remote(stats.at[other], stats.at[other], st_s.at[d - 1], st_r.at[other], (row, other)).wait_recv()
    total = stats[0]
    for c in range(1, ncol):
        total += stats[c]
    spread_out = jnp.concatenate([total] * (seq // 8), axis=0).T
    mean = spread_out[:, 0:1] / full
    spread = spread_out[:, 1:2] / full - mean * mean
    inv = lax.rsqrt(spread + 1e-05)
    gain = gain_ref[:, pl.ds(pl.multiple_of(col * width, 128), width)]

    for s in range(CHUNKS):
        rows = slice(s * ct, (s + 1) * ct)
        zbuf[s, z] = ((stream[rows, :] - mean[rows]) * inv[rows] * gain).astype(jnp.bfloat16)
        for d in range(1, nz):
            dev = (row, lax.rem(z + d, nz) * CORES + core)
            copy = remote(zbuf.at[s, z], zbuf.at[s, z], z_s.at[s, d - 1], z_r.at[s, z], dev)
            copy.start()
            sends.append((True, copy))

    if ratio % CORES == 0:
        mine = [CORES * i + core for i in range(ratio // CORES)]
        theirs = [CORES * i + 1 - core for i in range(ratio // CORES)]
        holds = lambda r: True
        lacks = lambda r: True
    else:
        mine, theirs = [0], [0]
        holds = lambda r: lax.rem(r, CORES) == core
        lacks = lambda r: lax.rem(r, CORES) != core

    def to_rows(s):
        for d in range(1, nz):
            other = lax.rem(z + d, nz)
            remote(
                zbuf.at[s, other], zbuf.at[s, other], z_s.at[s, d - 1], z_r.at[s, other],
                (row, other * CORES + core),
            ).wait_recv()
        for i, j in enumerate(mine):
            for d in range(1, nrow):
                to = lax.rem(row + d, nrow)
                copy = remote(
                    zbuf.at[s, lax.div(to * ratio + j, CORES)], xbuf.at[s, j, row],
                    p_s.at[s, i, d - 1], p_r.at[s, i, row], (to, col),
                )
                guarded(holds(to), copy.start)
                sends.append((holds(to), copy))

            def keep(j=j):
                xbuf[s, j, row] = zbuf[s, lax.div(row * ratio + j, CORES)]

            guarded(holds(row), keep)

    def to_sibling(s):
        for i, j in enumerate(mine):

            def pass_on(i=i, j=j):
                for d in range(1, nrow):
                    src = lax.rem(row + d, nrow)
                    remote(
                        xbuf.at[s, j, src], xbuf.at[s, j, src], p_s.at[s, i, d - 1], p_r.at[s, i, src],
                        (src, col),
                    ).wait_recv()
                remote(xbuf.at[s, j], xbuf.at[s, j], b_s.at[s, i], b_r.at[s, i], (row, sibling)).start()

            guarded(holds(row), pass_on)
            sends.append((
                holds(row),
                remote(xbuf.at[s, j], xbuf.at[s, j], b_s.at[s, i], b_r.at[s, i], (row, sibling)),
            ))

    def multiply(s):
        for i, j in enumerate(theirs):
            copy = remote(xbuf.at[s, j], xbuf.at[s, j], b_s.at[s, i], b_r.at[s, i], (row, sibling))
            guarded(lacks(row), copy.wait_recv)
        if s == 0:
            w_copy.wait()

        @pl.loop(0, cols // TILE)
        def _(n):
            at = pl.ds(pl.multiple_of(n * TILE, TILE), TILE)
            acc = None
            for j in range(ratio):
                term = jnp.dot(
                    xbuf[s, j].reshape(nrow * ct, width), w_ref[j * width:(j + 1) * width, at],
                    preferred_element_type=jnp.float32,
                )
                acc = term if acc is None else acc + term
            acc = acc.reshape(nrow, ct, TILE)
            acc_ref[...] = acc
            pbuf[s, :, :, at] = acc.astype(jnp.bfloat16)
            own[s, :, at] = acc_ref[row]

        for d in range(1, nrow):
            to = lax.rem(row + d, nrow)
            copy = remote(pbuf.at[s, to], rbuf.at[s, row], r_s.at[s, d - 1], r_r.at[s, row], (to, col))
            copy.start()
            sends.append((True, copy))

    def finish(s):
        for d in range(1, nrow):
            src = lax.rem(row + d, nrow)
            remote(
                pbuf.at[s, src], rbuf.at[s, src], r_s.at[s, d - 1], r_r.at[s, src], (src, col)
            ).wait_recv()

        @pl.loop(0, cols // TILE)
        def _(n):
            at = pl.ds(pl.multiple_of(n * TILE, TILE), TILE)
            u = own[s, :, at]
            for d in range(1, nrow):
                u = u + rbuf[s, lax.rem(row + d, nrow), :, at].astype(jnp.float32)
            u = 0.5 * u * (1.0 + jnp.tanh(math.sqrt(2.0 / math.pi) * (u + 0.044715 * (u * u * u))))
            out_ref[s * ct:(s + 1) * ct, at] = u.astype(jnp.bfloat16)

    to_rows(0)
    to_sibling(0)
    for s in range(CHUNKS):
        if s + 1 < CHUNKS:
            to_rows(s + 1)
        multiply(s)
        if s + 1 < CHUNKS:
            to_sibling(s + 1)
    for s in range(CHUNKS):
        finish(s)
    for cond, copy in sends:
        guarded(cond, copy.wait_send)


def per_device(q_seq, k_seq, v_seq, resid, ln_gain, w_up):
    nrow, ncol = lax.axis_size("row"), lax.axis_size("col")
    seq, width = q_seq.shape
    depth, cols = w_up.shape
    ratio, nz, ct = ncol // nrow, ncol // CORES, seq // CHUNKS
    per = max(1, ratio // CORES)
    dma = pltpu.SemaphoreType.DMA
    vmem = pl.BlockSpec(memory_space=pltpu.VMEM)
    return pl.pallas_call(
        functools.partial(kernel, nrow, ncol),
        out_shape=jax.ShapeDtypeStruct((seq, cols), jnp.bfloat16),
        in_specs=[vmem] * 5 + [pl.BlockSpec(memory_space=pl.ANY)],
        out_specs=vmem,
        scratch_shapes=[
            pltpu.VMEM((depth, cols), jnp.bfloat16),
            pltpu.VMEM((seq, width), jnp.float32),
            pltpu.VMEM((ncol, 8, seq), jnp.float32),
            pltpu.VMEM((CHUNKS, nz, ct, width), jnp.bfloat16),
            pltpu.VMEM((CHUNKS, ratio, nrow, ct, width), jnp.bfloat16),
            pltpu.VMEM((CHUNKS, nrow, ct, cols), jnp.bfloat16),
            pltpu.VMEM((CHUNKS, nrow, ct, cols), jnp.bfloat16),
            pltpu.VMEM((CHUNKS, ct, cols), jnp.float32),
            pltpu.VMEM((nrow, ct, TILE), jnp.float32),
            dma,
            dma((ncol - 1,)),
            dma((ncol,)),
            dma((CHUNKS, nz - 1)),
            dma((CHUNKS, nz)),
            dma((CHUNKS, per, nrow - 1)),
            dma((CHUNKS, per, nrow)),
            dma((CHUNKS, per)),
            dma((CHUNKS, per)),
            dma((CHUNKS, nrow - 1)),
            dma((CHUNKS, nrow)),
        ],
        compiler_params=pltpu.CompilerParams(
            collective_id=0, has_side_effects=True, vmem_limit_bytes=48 * 1024 * 1024
        ),
        cost_estimate=pl.CostEstimate(
            flops=2 * nrow * seq * depth * cols,
            bytes_accessed=2 * (depth * cols + seq * cols + 4 * seq * width),
            transcendentals=seq * cols,
        ),
    )(q_seq, k_seq, v_seq, resid, ln_gain.reshape(1, -1), w_up)


def solution(mesh):
    placed = (
        P("row", "col"),
        P("row", "col"),
        P("row", "col"),
        P("row", "col"),
        P(),
        P("row", "col"),
    )
    return jax.shard_map(
        per_device, mesh=mesh, in_specs=placed, out_specs=P("row", "col"), check_vma=False
    )
```

```python
import functools
import math

import jax
import jax.numpy as jnp
from jax import lax
from jax.experimental import pallas as pl
from jax.experimental.pallas import tpu as pltpu
from jax.sharding import PartitionSpec as P

HD = 128
CORES = 2
CHUNKS = 4
TILE = 512
MESH = pl.DeviceIdType.MESH


def guarded(cond, fn):
    if cond is True:
        fn()
    else:
        pl.when(cond)(fn)


def low_count(nrow):
    return max(n for n in range(1, math.isqrt(nrow) + 1) if nrow % n == 0)


def kernel(
    nrow, ncol,
    q_hbm, k_hbm, v_hbm, resid_hbm, gain_hbm, w_hbm, out_ref,
    q_ref, k_ref, v_ref, resid_ref, gain_ref, w_ref, stream, stats, zbuf, xbuf, acc_ref,
    one_p, one_r, one_own, two_p, two_r, two_own, other_one_p, other_one_r, other_one_own,
    other_two_p, other_two_r, other_two_own,
    in_sem, w_sem, st_s, st_r, z_s, z_r, p_s, p_r, b_s, b_r,
    r1_s, r1_r, r2_s, r2_r, q1_s, q1_r, q2_s, q2_r,
):
    seq, width = q_ref.shape
    cols = out_ref.shape[1]
    half = cols // 2
    tile = math.gcd(half, TILE)
    ratio = ncol // nrow
    nz = ncol // CORES
    ct = seq // CHUNKS
    full = width * ncol
    row, col = lax.axis_index("row"), lax.axis_index("col")
    z, core = lax.div(col, CORES), lax.rem(col, CORES)
    sibling = z * CORES + 1 - core
    sends = []

    def remote(src, dst, send_sem, recv_sem, dev):
        return pltpu.make_async_remote_copy(
            src_ref=src, dst_ref=dst, send_sem=send_sem, recv_sem=recv_sem,
            device_id=dev, device_id_type=MESH,
        )

    loads = [
        pltpu.make_async_copy(src, dst, in_sem.at[i])
        for i, (src, dst) in enumerate((
            (q_hbm, q_ref), (k_hbm, k_ref), (v_hbm, v_ref), (resid_hbm, resid_ref),
            (gain_hbm.at[:, pl.ds(pl.multiple_of(col * width, 128), width)], gain_ref),
        ))
    ]
    w_copy = pltpu.make_async_copy(w_hbm, w_ref, w_sem)
    for load in loads:
        load.start()
    w_copy.start()

    barrier = pltpu.get_barrier_semaphore()
    for d in range(1, ncol):
        pl.semaphore_signal(barrier, inc=1, device_id=(row, lax.rem(col + d, ncol)), device_id_type=MESH)
    for d in range(1, nrow):
        pl.semaphore_signal(barrier, inc=1, device_id=(lax.rem(row + d, nrow), col), device_id_type=MESH)

    for load in loads:
        load.wait()

    causal = lax.broadcasted_iota(jnp.int32, (seq, seq), 0) >= lax.broadcasted_iota(jnp.int32, (seq, seq), 1)
    s1 = jnp.zeros((seq, 1), jnp.float32)
    s2 = jnp.zeros((seq, 1), jnp.float32)
    for h in range(width // HD):
        cut = slice(h * HD, (h + 1) * HD)
        scores = lax.dot_general(
            q_ref[:, cut], k_ref[:, cut], (((1,), (1,)), ((), ())), preferred_element_type=jnp.float32
        ) * (1.0 / math.sqrt(HD))
        scores = jnp.where(causal, scores, -1e30)
        expo = jnp.exp(scores - jnp.max(scores, axis=-1, keepdims=True))
        prob = (expo / jnp.sum(expo, axis=-1, keepdims=True)).astype(jnp.bfloat16)
        attended = jnp.dot(prob, v_ref[:, cut], preferred_element_type=jnp.float32).astype(jnp.bfloat16)
        part = resid_ref[:, cut].astype(jnp.float32) + attended.astype(jnp.float32)
        stream[:, cut] = part
        s1 += jnp.sum(part, axis=1, keepdims=True)
        s2 += jnp.sum(part * part, axis=1, keepdims=True)

    lane = lax.broadcasted_iota(jnp.int32, (seq, HD), 1)
    packed = jnp.where(lane == 0, s1, jnp.where(lane == 1, s2, 0.0))
    stats[col] = packed.T[:8]
    pl.semaphore_wait(barrier, ncol + nrow - 2)
    for d in range(1, ncol):
        copy = remote(stats.at[col], stats.at[col], st_s.at[d - 1], st_r.at[col], (row, lax.rem(col + d, ncol)))
        copy.start()
        sends.append((True, copy))
    for d in range(1, ncol):
        other = lax.rem(col + d, ncol)
        remote(stats.at[other], stats.at[other], st_s.at[d - 1], st_r.at[other], (row, other)).wait_recv()
    total = stats[0]
    for c in range(1, ncol):
        total += stats[c]
    spread_out = jnp.concatenate([total] * (seq // 8), axis=0).T
    mean = spread_out[:, 0:1] / full
    spread = spread_out[:, 1:2] / full - mean * mean
    inv = lax.rsqrt(spread + 1e-05)
    gain = gain_ref[...]

    for s in range(CHUNKS):
        rows = slice(s * ct, (s + 1) * ct)
        zbuf[s, z] = ((stream[rows, :] - mean[rows]) * inv[rows] * gain).astype(jnp.bfloat16)
        for d in range(1, nz):
            dev = (row, lax.rem(z + d, nz) * CORES + core)
            copy = remote(zbuf.at[s, z], zbuf.at[s, z], z_s.at[s, d - 1], z_r.at[s, z], dev)
            copy.start()
            sends.append((True, copy))

    if ratio % CORES == 0:
        mine = [CORES * i + core for i in range(ratio // CORES)]
        theirs = [CORES * i + 1 - core for i in range(ratio // CORES)]
        holds = lambda r: True
        lacks = lambda r: True
    else:
        mine, theirs = [0], [0]
        holds = lambda r: lax.rem(r, CORES) == core
        lacks = lambda r: lax.rem(r, CORES) != core

    nlow = low_count(nrow)
    nhigh = nrow // nlow
    high, low_at = lax.div(row, nlow), lax.rem(row, nlow)
    ways = [
        dict(
            start=0, n1=nlow, n2=nhigh, one=low_at, two=high, index=lambda i, m: m * nlow + i,
            p1=one_p, r1=one_r, own1=one_own, p2=two_p, r2=two_r, own2=two_own,
            s1_s=r1_s, s1_r=r1_r, s2_s=r2_s, s2_r=r2_r,
        ),
        dict(
            start=half, n1=nhigh, n2=nlow, one=high, two=low_at, index=lambda i, m: i * nlow + m,
            p1=other_one_p, r1=other_one_r, own1=other_one_own, p2=other_two_p, r2=other_two_r,
            own2=other_two_own, s1_s=q1_s, s1_r=q1_r, s2_s=q2_s, s2_r=q2_r,
        ),
    ]

    def to_rows(s):
        for d in range(1, nz):
            other = lax.rem(z + d, nz)
            remote(
                zbuf.at[s, other], zbuf.at[s, other], z_s.at[s, d - 1], z_r.at[s, other],
                (row, other * CORES + core),
            ).wait_recv()
        for i, j in enumerate(mine):
            for d in range(1, nrow):
                to = lax.rem(row + d, nrow)
                copy = remote(
                    zbuf.at[s, lax.div(to * ratio + j, CORES)], xbuf.at[s, j, row],
                    p_s.at[s, i, d - 1], p_r.at[s, i, row], (to, col),
                )
                guarded(holds(to), copy.start)
                sends.append((holds(to), copy))

            def keep(j=j):
                xbuf[s, j, row] = zbuf[s, lax.div(row * ratio + j, CORES)]

            guarded(holds(row), keep)

    def to_sibling(s):
        for i, j in enumerate(mine):

            def pass_on(i=i, j=j):
                for d in range(1, nrow):
                    src = lax.rem(row + d, nrow)
                    remote(
                        xbuf.at[s, j, src], xbuf.at[s, j, src], p_s.at[s, i, d - 1], p_r.at[s, i, src],
                        (src, col),
                    ).wait_recv()
                remote(xbuf.at[s, j], xbuf.at[s, j], b_s.at[s, i], b_r.at[s, i], (row, sibling)).start()

            guarded(holds(row), pass_on)
            sends.append((
                holds(row),
                remote(xbuf.at[s, j], xbuf.at[s, j], b_s.at[s, i], b_r.at[s, i], (row, sibling)),
            ))

    def multiply(s):
        for i, j in enumerate(theirs):
            copy = remote(xbuf.at[s, j], xbuf.at[s, j], b_s.at[s, i], b_r.at[s, i], (row, sibling))
            guarded(lacks(row), copy.wait_recv)
        if s == 0:
            w_copy.wait()

        for way in ways:
            start, one, p, kept = way["start"], way["one"], way["p1"], way["own1"]

            @pl.loop(0, half // tile)
            def _(n):
                at = pl.ds(pl.multiple_of(n * tile, tile), tile)
                w_at = pl.ds(pl.multiple_of(start + n * tile, tile), tile)
                acc = None
                for j in range(ratio):
                    term = jnp.dot(
                        xbuf[s, j].reshape(nrow * ct, width), w_ref[j * width:(j + 1) * width, w_at],
                        preferred_element_type=jnp.float32,
                    )
                    acc = term if acc is None else acc + term
                acc = acc.reshape(nrow, ct, tile)
                acc_ref[...] = acc
                low = acc.astype(jnp.bfloat16)
                for i in range(way["n1"]):
                    for m in range(way["n2"]):
                        p[s, i, m, :, at] = low[way["index"](i, m)]
                for m in range(way["n2"]):
                    kept[s, m, :, at] = acc_ref[way["index"](one, m)]

            for d in range(1, way["n1"]):
                to = lax.rem(one + d, way["n1"])
                copy = remote(
                    p.at[s, to], way["r1"].at[s, one], way["s1_s"].at[s, d - 1], way["s1_r"].at[s, one],
                    (way["index"](to, way["two"]), col),
                )
                copy.start()
                sends.append((True, copy))

    def add_first(s):
        for way in ways:
            one, two = way["one"], way["two"]
            for d in range(1, way["n1"]):
                src = lax.rem(one + d, way["n1"])
                remote(
                    way["p1"].at[s, src], way["r1"].at[s, src], way["s1_s"].at[s, d - 1], way["s1_r"].at[s, src],
                    (way["index"](src, two), col),
                ).wait_recv()
            for e in list(range(1, way["n2"])) + [0]:
                to = lax.rem(two + e, way["n2"])

                @pl.loop(0, half // tile)
                def _(n):
                    at = pl.ds(pl.multiple_of(n * tile, tile), tile)
                    u = way["own1"][s, to, :, at]
                    for d in range(1, way["n1"]):
                        u = u + way["r1"][s, lax.rem(one + d, way["n1"]), to, :, at].astype(jnp.float32)
                    if e:
                        way["p2"][s, to, :, at] = u.astype(jnp.bfloat16)
                    else:
                        way["own2"][s, :, at] = u

                if e:
                    copy = remote(
                        way["p2"].at[s, to], way["r2"].at[s, two], way["s2_s"].at[s, e - 1],
                        way["s2_r"].at[s, two], (way["index"](one, to), col),
                    )
                    copy.start()
                    sends.append((True, copy))

    def finish(s):
        for way in ways:
            one, two = way["one"], way["two"]
            for e in range(1, way["n2"]):
                src = lax.rem(two + e, way["n2"])
                remote(
                    way["p2"].at[s, src], way["r2"].at[s, src], way["s2_s"].at[s, e - 1],
                    way["s2_r"].at[s, src], (way["index"](one, src), col),
                ).wait_recv()

            @pl.loop(0, half // tile)
            def _(n):
                at = pl.ds(pl.multiple_of(n * tile, tile), tile)
                u = way["own2"][s, :, at]
                for e in range(1, way["n2"]):
                    u = u + way["r2"][s, lax.rem(two + e, way["n2"]), :, at].astype(jnp.float32)
                u = 0.5 * u * (1.0 + jnp.tanh(math.sqrt(2.0 / math.pi) * (u + 0.044715 * (u * u * u))))
                w_at = pl.ds(pl.multiple_of(way["start"] + n * tile, tile), tile)
                out_ref[s * ct:(s + 1) * ct, w_at] = u.astype(jnp.bfloat16)

    to_rows(0)
    to_sibling(0)
    for s in range(CHUNKS):
        if s + 1 < CHUNKS:
            to_rows(s + 1)
        multiply(s)
        if s + 1 < CHUNKS:
            to_sibling(s + 1)
        if s:
            add_first(s - 1)
    for s in range(CHUNKS - 2):
        finish(s)
    add_first(CHUNKS - 1)
    for s in range(max(CHUNKS - 2, 0), CHUNKS):
        finish(s)
    for cond, copy in sends:
        guarded(cond, copy.wait_send)


def per_device(q_seq, k_seq, v_seq, resid, ln_gain, w_up):
    nrow, ncol = lax.axis_size("row"), lax.axis_size("col")
    seq, width = q_seq.shape
    depth, cols = w_up.shape
    ratio, nz, ct = ncol // nrow, ncol // CORES, seq // CHUNKS
    per = max(1, ratio // CORES)
    dma = pltpu.SemaphoreType.DMA
    vmem = pl.BlockSpec(memory_space=pltpu.VMEM)
    half = cols // 2
    tile = math.gcd(half, TILE)
    nlow = low_count(nrow)
    nhigh = nrow // nlow

    def sums(n1, n2):
        return [
            pltpu.VMEM((CHUNKS, n1, n2, ct, half), jnp.bfloat16),
            pltpu.VMEM((CHUNKS, n1, n2, ct, half), jnp.bfloat16),
            pltpu.VMEM((CHUNKS, n2, ct, half), jnp.float32),
            pltpu.VMEM((CHUNKS, n2, ct, half), jnp.bfloat16),
            pltpu.VMEM((CHUNKS, n2, ct, half), jnp.bfloat16),
            pltpu.VMEM((CHUNKS, ct, half), jnp.float32),
        ]

    return pl.pallas_call(
        functools.partial(kernel, nrow, ncol),
        out_shape=jax.ShapeDtypeStruct((seq, cols), jnp.bfloat16),
        in_specs=[pl.BlockSpec(memory_space=pltpu.HBM)] * 6,
        out_specs=vmem,
        scratch_shapes=[
            *[pltpu.VMEM((seq, width), jnp.bfloat16)] * 4,
            pltpu.VMEM((1, width), jnp.float32),
            pltpu.VMEM((depth, cols), jnp.bfloat16),
            pltpu.VMEM((seq, width), jnp.float32),
            pltpu.VMEM((ncol, 8, seq), jnp.float32),
            pltpu.VMEM((CHUNKS, nz, ct, width), jnp.bfloat16),
            pltpu.VMEM((CHUNKS, ratio, nrow, ct, width), jnp.bfloat16),
            pltpu.VMEM((nrow, ct, tile), jnp.float32),
            *sums(nlow, nhigh),
            *sums(nhigh, nlow),
            dma((5,)),
            dma,
            dma((ncol - 1,)),
            dma((ncol,)),
            dma((CHUNKS, nz - 1)),
            dma((CHUNKS, nz)),
            dma((CHUNKS, per, nrow - 1)),
            dma((CHUNKS, per, nrow)),
            dma((CHUNKS, per)),
            dma((CHUNKS, per)),
            dma((CHUNKS, nlow)),
            dma((CHUNKS, nlow)),
            dma((CHUNKS, nhigh)),
            dma((CHUNKS, nhigh)),
            dma((CHUNKS, nhigh)),
            dma((CHUNKS, nhigh)),
            dma((CHUNKS, nlow)),
            dma((CHUNKS, nlow)),
        ],
        compiler_params=pltpu.CompilerParams(
            collective_id=0, has_side_effects=True, vmem_limit_bytes=48 * 1024 * 1024
        ),
        cost_estimate=pl.CostEstimate(
            flops=2 * nrow * seq * depth * cols,
            bytes_accessed=2 * (depth * cols + seq * cols + 4 * seq * width),
            transcendentals=seq * cols,
        ),
    )(q_seq, k_seq, v_seq, resid, ln_gain.reshape(1, -1), w_up)


def solution(mesh):
    placed = (
        P("row", "col"),
        P("row", "col"),
        P("row", "col"),
        P("row", "col"),
        P(),
        P("row", "col"),
    )
    return jax.shard_map(
        per_device, mesh=mesh, in_specs=placed, out_specs=P("row", "col"), check_vma=False
    )
```

```python
import functools
import math

import jax
import jax.numpy as jnp
from jax import lax
from jax.experimental import pallas as pl
from jax.experimental.pallas import tpu as pltpu
from jax.sharding import PartitionSpec as P

HD = 128
CORES = 2
CHUNKS = 8
GROUP = 3
TILE = 512
MESH = pl.DeviceIdType.MESH


def guarded(cond, fn):
    if cond is True:
        fn()
    else:
        pl.when(cond)(fn)


def low_count(nrow):
    return max(n for n in range(1, math.isqrt(nrow) + 1) if nrow % n == 0)


def kernel(
    nrow, ncol,
    q_hbm, k_hbm, v_hbm, resid_hbm, gain_hbm, w_hbm, out_hbm,
    q_ref, k_ref, v_ref, resid_ref, gain_ref, w_ref, stream, stats, zbuf, xbuf, acc_ref, out_ref,
    one_p, one_r, one_own, two_p, two_r, two_own, other_one_p, other_one_r, other_one_own,
    other_two_p, other_two_r, other_two_own,
    in_sem, w_sem, st_s, st_r, z_s, z_r, p_s, p_r, b_s, b_r,
    out_sem, r1_s, r1_r, r2_s, r2_r, q1_s, q1_r, q2_s, q2_r,
):
    seq, width = q_ref.shape
    cols = out_ref.shape[2]
    half = cols // 2
    tile = math.gcd(half, TILE)
    ratio = ncol // nrow
    nz = ncol // CORES
    ct = seq // CHUNKS
    full = width * ncol
    row, col = lax.axis_index("row"), lax.axis_index("col")
    z, core = lax.div(col, CORES), lax.rem(col, CORES)
    sibling = z * CORES + 1 - core
    sends = []
    stores = []

    def remote(src, dst, send_sem, recv_sem, dev):
        return pltpu.make_async_remote_copy(
            src_ref=src, dst_ref=dst, send_sem=send_sem, recv_sem=recv_sem,
            device_id=dev, device_id_type=MESH,
        )

    loads = [
        pltpu.make_async_copy(src, dst, in_sem.at[i])
        for i, (src, dst) in enumerate((
            (q_hbm, q_ref), (k_hbm, k_ref), (v_hbm, v_ref), (resid_hbm, resid_ref),
            (gain_hbm.at[:, pl.ds(pl.multiple_of(col * width, 128), width)], gain_ref),
        ))
    ]
    w_copy = pltpu.make_async_copy(w_hbm, w_ref, w_sem)
    for load in loads:
        load.start()
    w_copy.start()

    barrier = pltpu.get_barrier_semaphore()
    for d in range(1, ncol):
        pl.semaphore_signal(barrier, inc=1, device_id=(row, lax.rem(col + d, ncol)), device_id_type=MESH)
    for d in range(1, nrow):
        pl.semaphore_signal(barrier, inc=1, device_id=(lax.rem(row + d, nrow), col), device_id_type=MESH)

    for load in loads:
        load.wait()

    causal = lax.broadcasted_iota(jnp.int32, (seq, seq), 0) >= lax.broadcasted_iota(jnp.int32, (seq, seq), 1)
    sum1 = jnp.zeros((seq, HD), jnp.float32)
    sum2 = jnp.zeros((seq, HD), jnp.float32)
    heads = width // HD
    for first in range(0, heads, GROUP):
        cuts = [slice(h * HD, (h + 1) * HD) for h in range(first, min(first + GROUP, heads))]
        scores = [
            lax.dot_general(
                q_ref[:, cut], k_ref[:, cut], (((1,), (1,)), ((), ())), preferred_element_type=jnp.float32
            ) * (1.0 / math.sqrt(HD))
            for cut in cuts
        ]
        scores = [jnp.where(causal, x, -1e30) for x in scores]
        highest = [jnp.max(x, axis=-1, keepdims=True) for x in scores]
        expo = [jnp.exp(x - m) for x, m in zip(scores, highest)]
        below = [jnp.sum(x, axis=-1, keepdims=True) for x in expo]
        prob = [(x / m).astype(jnp.bfloat16) for x, m in zip(expo, below)]
        attended = [
            jnp.dot(x, v_ref[:, cut], preferred_element_type=jnp.float32).astype(jnp.bfloat16)
            for x, cut in zip(prob, cuts)
        ]
        for x, cut in zip(attended, cuts):
            part = resid_ref[:, cut].astype(jnp.float32) + x.astype(jnp.float32)
            stream[:, cut] = part
            sum1 += part
            sum2 += part * part

    place = lax.broadcasted_iota(jnp.int32, (8, seq), 0)
    stats[col] = jnp.where(
        place == 0,
        jnp.sum(sum1.T, axis=0, keepdims=True),
        jnp.where(place == 1, jnp.sum(sum2.T, axis=0, keepdims=True), 0.0),
    )
    pl.semaphore_wait(barrier, ncol + nrow - 2)
    for d in range(1, ncol):
        copy = remote(stats.at[col], stats.at[col], st_s.at[d - 1], st_r.at[col], (row, lax.rem(col + d, ncol)))
        copy.start()
        sends.append((True, copy))
    for d in range(1, ncol):
        other = lax.rem(col + d, ncol)
        remote(stats.at[other], stats.at[other], st_s.at[d - 1], st_r.at[other], (row, other)).wait_recv()
    total = stats[0]
    for c in range(1, ncol):
        total += stats[c]
    spread_out = jnp.concatenate([total] * (seq // 8), axis=0).T
    mean = spread_out[:, 0:1] / full
    spread = spread_out[:, 1:2] / full - mean * mean
    inv = lax.rsqrt(spread + 1e-05)
    gain = gain_ref[...]

    for s in range(CHUNKS):
        rows = slice(s * ct, (s + 1) * ct)
        zbuf[s, z] = ((stream[rows, :] - mean[rows]) * inv[rows] * gain).astype(jnp.bfloat16)
        for d in range(1, nz):
            dev = (row, lax.rem(z + d, nz) * CORES + core)
            copy = remote(zbuf.at[s, z], zbuf.at[s, z], z_s.at[s, d - 1], z_r.at[s, z], dev)
            copy.start()
            sends.append((True, copy))

    if ratio % CORES == 0:
        mine = [CORES * i + core for i in range(ratio // CORES)]
        theirs = [CORES * i + 1 - core for i in range(ratio // CORES)]
        holds = lambda r: True
        lacks = lambda r: True
    else:
        mine, theirs = [0], [0]
        holds = lambda r: lax.rem(r, CORES) == core
        lacks = lambda r: lax.rem(r, CORES) != core

    nlow = low_count(nrow)
    nhigh = nrow // nlow
    high, low_at = lax.div(row, nlow), lax.rem(row, nlow)
    ways = [
        dict(
            start=0, n1=nlow, n2=nhigh, one=low_at, two=high, index=lambda i, m: m * nlow + i,
            p1=one_p, r1=one_r, own1=one_own, p2=two_p, r2=two_r, own2=two_own,
            s1_s=r1_s, s1_r=r1_r, s2_s=r2_s, s2_r=r2_r,
        ),
        dict(
            start=half, n1=nhigh, n2=nlow, one=high, two=low_at, index=lambda i, m: i * nlow + m,
            p1=other_one_p, r1=other_one_r, own1=other_one_own, p2=other_two_p, r2=other_two_r,
            own2=other_two_own, s1_s=q1_s, s1_r=q1_r, s2_s=q2_s, s2_r=q2_r,
        ),
    ]

    def to_rows(s):
        for d in range(1, nz):
            other = lax.rem(z + d, nz)
            remote(
                zbuf.at[s, other], zbuf.at[s, other], z_s.at[s, d - 1], z_r.at[s, other],
                (row, other * CORES + core),
            ).wait_recv()
        for i, j in enumerate(mine):
            for d in range(1, nrow):
                to = lax.rem(row + d, nrow)
                copy = remote(
                    zbuf.at[s, lax.div(to * ratio + j, CORES)], xbuf.at[s, j, row],
                    p_s.at[s, i, d - 1], p_r.at[s, i, row], (to, col),
                )
                guarded(holds(to), copy.start)
                sends.append((holds(to), copy))

            def keep(j=j):
                xbuf[s, j, row] = zbuf[s, lax.div(row * ratio + j, CORES)]

            guarded(holds(row), keep)

    def to_sibling(s):
        for i, j in enumerate(mine):

            def pass_on(i=i, j=j):
                for d in range(1, nrow):
                    src = lax.rem(row + d, nrow)
                    remote(
                        xbuf.at[s, j, src], xbuf.at[s, j, src], p_s.at[s, i, d - 1], p_r.at[s, i, src],
                        (src, col),
                    ).wait_recv()
                remote(xbuf.at[s, j], xbuf.at[s, j], b_s.at[s, i], b_r.at[s, i], (row, sibling)).start()

            guarded(holds(row), pass_on)
            sends.append((
                holds(row),
                remote(xbuf.at[s, j], xbuf.at[s, j], b_s.at[s, i], b_r.at[s, i], (row, sibling)),
            ))

    def multiply(s):
        for i, j in enumerate(theirs):
            copy = remote(xbuf.at[s, j], xbuf.at[s, j], b_s.at[s, i], b_r.at[s, i], (row, sibling))
            guarded(lacks(row), copy.wait_recv)
        if s == 0:
            w_copy.wait()

        for way in ways:
            start, one, p, kept = way["start"], way["one"], way["p1"], way["own1"]

            @pl.loop(0, half // tile)
            def _(n):
                at = pl.ds(pl.multiple_of(n * tile, tile), tile)
                w_at = pl.ds(pl.multiple_of(start + n * tile, tile), tile)
                acc = None
                for j in range(ratio):
                    term = jnp.dot(
                        xbuf[s, j].reshape(nrow * ct, width), w_ref[j * width:(j + 1) * width, w_at],
                        preferred_element_type=jnp.float32,
                    )
                    acc = term if acc is None else acc + term
                acc = acc.reshape(nrow, ct, tile)
                acc_ref[...] = acc
                low = acc.astype(jnp.bfloat16)
                for i in range(way["n1"]):
                    for m in range(way["n2"]):
                        p[s, i, m, :, at] = low[way["index"](i, m)]
                for m in range(way["n2"]):
                    kept[s, m, :, at] = acc_ref[way["index"](one, m)]

            for d in range(1, way["n1"]):
                to = lax.rem(one + d, way["n1"])
                copy = remote(
                    p.at[s, to], way["r1"].at[s, one], way["s1_s"].at[s, d - 1], way["s1_r"].at[s, one],
                    (way["index"](to, way["two"]), col),
                )
                copy.start()
                sends.append((True, copy))

    def add_first(s):
        for way in ways:
            one, two = way["one"], way["two"]
            for d in range(1, way["n1"]):
                src = lax.rem(one + d, way["n1"])
                remote(
                    way["p1"].at[s, src], way["r1"].at[s, src], way["s1_s"].at[s, d - 1], way["s1_r"].at[s, src],
                    (way["index"](src, two), col),
                ).wait_recv()
            for e in list(range(1, way["n2"])) + [0]:
                to = lax.rem(two + e, way["n2"])

                @pl.loop(0, half // tile)
                def _(n):
                    at = pl.ds(pl.multiple_of(n * tile, tile), tile)
                    u = way["own1"][s, to, :, at]
                    for d in range(1, way["n1"]):
                        u = u + way["r1"][s, lax.rem(one + d, way["n1"]), to, :, at].astype(jnp.float32)
                    if e:
                        way["p2"][s, to, :, at] = u.astype(jnp.bfloat16)
                    else:
                        way["own2"][s, :, at] = u

                if e:
                    copy = remote(
                        way["p2"].at[s, to], way["r2"].at[s, two], way["s2_s"].at[s, e - 1],
                        way["s2_r"].at[s, two], (way["index"](one, to), col),
                    )
                    copy.start()
                    sends.append((True, copy))

    def finish(s):
        for way in ways:
            one, two = way["one"], way["two"]
            for e in range(1, way["n2"]):
                src = lax.rem(two + e, way["n2"])
                remote(
                    way["p2"].at[s, src], way["r2"].at[s, src], way["s2_s"].at[s, e - 1],
                    way["s2_r"].at[s, src], (way["index"](one, src), col),
                ).wait_recv()

            @pl.loop(0, half // tile)
            def _(n):
                at = pl.ds(pl.multiple_of(n * tile, tile), tile)
                u = way["own2"][s, :, at]
                for e in range(1, way["n2"]):
                    u = u + way["r2"][s, lax.rem(two + e, way["n2"]), :, at].astype(jnp.float32)
                u = 0.5 * u * (1.0 + jnp.tanh(math.sqrt(2.0 / math.pi) * (u + 0.044715 * (u * u * u))))
                w_at = pl.ds(pl.multiple_of(way["start"] + n * tile, tile), tile)
                out_ref[s, :, w_at] = u.astype(jnp.bfloat16)

        copy = pltpu.make_async_copy(out_ref.at[s], out_hbm.at[s * ct:(s + 1) * ct, :], out_sem.at[s])
        copy.start()
        stores.append(copy)

    to_rows(0)
    to_sibling(0)
    for s in range(CHUNKS):
        if s + 1 < CHUNKS:
            to_rows(s + 1)
        multiply(s)
        if s + 1 < CHUNKS:
            to_sibling(s + 1)
        if s:
            add_first(s - 1)
    for s in range(CHUNKS - 2):
        finish(s)
    add_first(CHUNKS - 1)
    for s in range(max(CHUNKS - 2, 0), CHUNKS):
        finish(s)
    for cond, copy in sends:
        guarded(cond, copy.wait_send)
    for copy in stores:
        copy.wait()


def per_device(q_seq, k_seq, v_seq, resid, ln_gain, w_up):
    nrow, ncol = lax.axis_size("row"), lax.axis_size("col")
    seq, width = q_seq.shape
    depth, cols = w_up.shape
    ratio, nz, ct = ncol // nrow, ncol // CORES, seq // CHUNKS
    per = max(1, ratio // CORES)
    dma = pltpu.SemaphoreType.DMA
    hbm = pl.BlockSpec(memory_space=pltpu.HBM)
    half = cols // 2
    tile = math.gcd(half, TILE)
    nlow = low_count(nrow)
    nhigh = nrow // nlow

    def sums(n1, n2):
        return [
            pltpu.VMEM((CHUNKS, n1, n2, ct, half), jnp.bfloat16),
            pltpu.VMEM((CHUNKS, n1, n2, ct, half), jnp.bfloat16),
            pltpu.VMEM((CHUNKS, n2, ct, half), jnp.float32),
            pltpu.VMEM((CHUNKS, n2, ct, half), jnp.bfloat16),
            pltpu.VMEM((CHUNKS, n2, ct, half), jnp.bfloat16),
            pltpu.VMEM((CHUNKS, ct, half), jnp.float32),
        ]

    return pl.pallas_call(
        functools.partial(kernel, nrow, ncol),
        out_shape=jax.ShapeDtypeStruct((seq, cols), jnp.bfloat16),
        in_specs=[hbm] * 6,
        out_specs=hbm,
        scratch_shapes=[
            *[pltpu.VMEM((seq, width), jnp.bfloat16)] * 4,
            pltpu.VMEM((1, width), jnp.float32),
            pltpu.VMEM((depth, cols), jnp.bfloat16),
            pltpu.VMEM((seq, width), jnp.float32),
            pltpu.VMEM((ncol, 8, seq), jnp.float32),
            pltpu.VMEM((CHUNKS, nz, ct, width), jnp.bfloat16),
            pltpu.VMEM((CHUNKS, ratio, nrow, ct, width), jnp.bfloat16),
            pltpu.VMEM((nrow, ct, tile), jnp.float32),
            pltpu.VMEM((CHUNKS, ct, cols), jnp.bfloat16),
            *sums(nlow, nhigh),
            *sums(nhigh, nlow),
            dma((5,)),
            dma,
            dma((ncol - 1,)),
            dma((ncol,)),
            dma((CHUNKS, nz - 1)),
            dma((CHUNKS, nz)),
            dma((CHUNKS, per, nrow - 1)),
            dma((CHUNKS, per, nrow)),
            dma((CHUNKS, per)),
            dma((CHUNKS, per)),
            dma((CHUNKS,)),
            dma((CHUNKS, nlow)),
            dma((CHUNKS, nlow)),
            dma((CHUNKS, nhigh)),
            dma((CHUNKS, nhigh)),
            dma((CHUNKS, nhigh)),
            dma((CHUNKS, nhigh)),
            dma((CHUNKS, nlow)),
            dma((CHUNKS, nlow)),
        ],
        compiler_params=pltpu.CompilerParams(
            collective_id=0, has_side_effects=True, vmem_limit_bytes=60 * 1024 * 1024
        ),
        cost_estimate=pl.CostEstimate(
            flops=2 * nrow * seq * depth * cols,
            bytes_accessed=2 * (depth * cols + seq * cols + 4 * seq * width),
            transcendentals=seq * cols,
        ),
    )(q_seq, k_seq, v_seq, resid, ln_gain.reshape(1, -1), w_up)


def solution(mesh):
    placed = (
        P("row", "col"),
        P("row", "col"),
        P("row", "col"),
        P("row", "col"),
        P(),
        P("row", "col"),
    )
    return jax.shard_map(
        per_device, mesh=mesh, in_specs=placed, out_specs=P("row", "col"), check_vma=False
    )
```

```python
import functools
import math

import jax
import jax.numpy as jnp
from jax import lax
from jax.experimental import pallas as pl
from jax.experimental.pallas import tpu as pltpu
from jax.sharding import PartitionSpec as P

HD = 128
CORES = 2
CHUNKS = 4
SPANS = ((0, 1), (1, 2), (2, 4))
GROUP = 3
TILE = 512
MESH = pl.DeviceIdType.MESH


def guarded(cond, fn):
    if cond is True:
        fn()
    else:
        pl.when(cond)(fn)


def low_count(nrow):
    return max(n for n in range(1, math.isqrt(nrow) + 1) if nrow % n == 0)


def kernel(
    nrow, ncol,
    q_hbm, k_hbm, v_hbm, resid_hbm, gain_hbm, w_hbm, out_ref,
    q_ref, k_ref, v_ref, resid_ref, gain_ref, w_ref, stream, stats, zbuf, xbuf, acc_ref,
    one_p, one_r, one_own, two_p, two_r, two_own, other_one_p, other_one_r, other_one_own,
    other_two_p, other_two_r, other_two_own,
    in_sem, w_sem, st_s, st_r, z_s, z_r, p_s, p_r, b_s, b_r,
    r1_s, r1_r, r2_s, r2_r, q1_s, q1_r, q2_s, q2_r,
):
    seq, width = q_ref.shape
    cols = out_ref.shape[1]
    half = cols // 2
    tile = math.gcd(half, TILE)
    ratio = ncol // nrow
    nz = ncol // CORES
    ct = seq // CHUNKS
    full = width * ncol
    row, col = lax.axis_index("row"), lax.axis_index("col")
    z, core = lax.div(col, CORES), lax.rem(col, CORES)
    sibling = z * CORES + 1 - core
    sends = []

    def remote(src, dst, send_sem, recv_sem, dev):
        return pltpu.make_async_remote_copy(
            src_ref=src, dst_ref=dst, send_sem=send_sem, recv_sem=recv_sem,
            device_id=dev, device_id_type=MESH,
        )

    loads = [
        pltpu.make_async_copy(src, dst, in_sem.at[i])
        for i, (src, dst) in enumerate((
            (q_hbm, q_ref), (k_hbm, k_ref), (v_hbm, v_ref), (resid_hbm, resid_ref),
            (gain_hbm.at[:, pl.ds(pl.multiple_of(col * width, 128), width)], gain_ref),
        ))
    ]
    w_copy = pltpu.make_async_copy(w_hbm, w_ref, w_sem)
    for load in loads:
        load.start()
    w_copy.start()

    barrier = pltpu.get_barrier_semaphore()
    for d in range(1, ncol):
        pl.semaphore_signal(barrier, inc=1, device_id=(row, lax.rem(col + d, ncol)), device_id_type=MESH)
    for d in range(1, nrow):
        pl.semaphore_signal(barrier, inc=1, device_id=(lax.rem(row + d, nrow), col), device_id_type=MESH)

    for load in loads:
        load.wait()

    causal = lax.broadcasted_iota(jnp.int32, (seq, seq), 0) >= lax.broadcasted_iota(jnp.int32, (seq, seq), 1)
    sum1 = jnp.zeros((seq, HD), jnp.float32)
    sum2 = jnp.zeros((seq, HD), jnp.float32)
    heads = width // HD
    for first in range(0, heads, GROUP):
        cuts = [slice(h * HD, (h + 1) * HD) for h in range(first, min(first + GROUP, heads))]
        scores = [
            lax.dot_general(
                q_ref[:, cut], k_ref[:, cut], (((1,), (1,)), ((), ())), preferred_element_type=jnp.float32
            ) * (1.0 / math.sqrt(HD))
            for cut in cuts
        ]
        scores = [jnp.where(causal, x, -1e30) for x in scores]
        highest = [jnp.max(x, axis=-1, keepdims=True) for x in scores]
        expo = [jnp.exp(x - m) for x, m in zip(scores, highest)]
        below = [jnp.sum(x, axis=-1, keepdims=True) for x in expo]
        prob = [(x / m).astype(jnp.bfloat16) for x, m in zip(expo, below)]
        attended = [
            jnp.dot(x, v_ref[:, cut], preferred_element_type=jnp.float32).astype(jnp.bfloat16)
            for x, cut in zip(prob, cuts)
        ]
        for x, cut in zip(attended, cuts):
            part = resid_ref[:, cut].astype(jnp.float32) + x.astype(jnp.float32)
            stream[:, cut] = part
            sum1 += part
            sum2 += part * part

    place = lax.broadcasted_iota(jnp.int32, (8, seq), 0)
    stats[col] = jnp.where(
        place == 0,
        jnp.sum(sum1.T, axis=0, keepdims=True),
        jnp.where(place == 1, jnp.sum(sum2.T, axis=0, keepdims=True), 0.0),
    )
    pl.semaphore_wait(barrier, ncol + nrow - 2)
    for d in range(1, ncol):
        copy = remote(stats.at[col], stats.at[col], st_s.at[d - 1], st_r.at[col], (row, lax.rem(col + d, ncol)))
        copy.start()
        sends.append((True, copy))
    for d in range(1, ncol):
        other = lax.rem(col + d, ncol)
        remote(stats.at[other], stats.at[other], st_s.at[d - 1], st_r.at[other], (row, other)).wait_recv()
    total = stats[0]
    for c in range(1, ncol):
        total += stats[c]
    spread_out = jnp.concatenate([total] * (seq // 8), axis=0).T
    mean = spread_out[:, 0:1] / full
    spread = spread_out[:, 1:2] / full - mean * mean
    inv = lax.rsqrt(spread + 1e-05)
    gain = gain_ref[...]

    def along_z(s):
        copies = []
        for d in range(1, nz):
            dev = (row, lax.rem(z + d, nz) * CORES + core)
            copy = remote(zbuf.at[s, z], zbuf.at[s, z], z_s.at[s, d - 1], z_r.at[s, z], dev)
            copy.start()
            copies.append(copy)
        return copies

    def normalize(s):
        rows = slice(s * ct, (s + 1) * ct)
        zbuf[s, z] = ((stream[rows, :] - mean[rows]) * inv[rows] * gain).astype(jnp.bfloat16)

    normalize(0)
    leaving = [along_z(0)]
    for s in range(1, CHUNKS):
        normalize(s)

    if ratio % CORES == 0:
        mine = [CORES * i + core for i in range(ratio // CORES)]
        theirs = [CORES * i + 1 - core for i in range(ratio // CORES)]
        holds = lambda r: True
        lacks = lambda r: True
    else:
        mine, theirs = [0], [0]
        holds = lambda r: lax.rem(r, CORES) == core
        lacks = lambda r: lax.rem(r, CORES) != core

    nlow = low_count(nrow)
    nhigh = nrow // nlow
    high, low_at = lax.div(row, nlow), lax.rem(row, nlow)
    ways = [
        dict(
            start=0, n1=nlow, n2=nhigh, one=low_at, two=high, index=lambda i, m: m * nlow + i,
            p1=one_p, r1=one_r, own1=one_own, p2=two_p, r2=two_r, own2=two_own,
            s1_s=r1_s, s1_r=r1_r, s2_s=r2_s, s2_r=r2_r,
        ),
        dict(
            start=half, n1=nhigh, n2=nlow, one=high, two=low_at, index=lambda i, m: i * nlow + m,
            p1=other_one_p, r1=other_one_r, own1=other_one_own, p2=other_two_p, r2=other_two_r,
            own2=other_two_own, s1_s=q1_s, s1_r=q1_r, s2_s=q2_s, s2_r=q2_r,
        ),
    ]

    def to_rows(s):
        for copy in leaving[s]:
            copy.wait_send()
        if s + 1 < CHUNKS:
            leaving.append(along_z(s + 1))
        for d in range(1, nz):
            other = lax.rem(z + d, nz)
            remote(
                zbuf.at[s, other], zbuf.at[s, other], z_s.at[s, d - 1], z_r.at[s, other],
                (row, other * CORES + core),
            ).wait_recv()
        for i, j in enumerate(mine):
            for d in range(1, nrow):
                to = lax.rem(row + d, nrow)
                copy = remote(
                    zbuf.at[s, lax.div(to * ratio + j, CORES)], xbuf.at[j, s, row],
                    p_s.at[s, i, d - 1], p_r.at[s, i, row], (to, col),
                )
                guarded(holds(to), copy.start)
                sends.append((holds(to), copy))

            def keep(j=j):
                xbuf[j, s, row] = zbuf[s, lax.div(row * ratio + j, CORES)]

            guarded(holds(row), keep)

    def to_sibling(s):
        for i, j in enumerate(mine):

            def pass_on(i=i, j=j):
                for d in range(1, nrow):
                    src = lax.rem(row + d, nrow)
                    remote(
                        xbuf.at[j, s, src], xbuf.at[j, s, src], p_s.at[s, i, d - 1], p_r.at[s, i, src],
                        (src, col),
                    ).wait_recv()
                remote(xbuf.at[j, s], xbuf.at[j, s], b_s.at[s, i], b_r.at[s, i], (row, sibling)).start()

            guarded(holds(row), pass_on)
            sends.append((
                holds(row),
                remote(xbuf.at[j, s], xbuf.at[j, s], b_s.at[s, i], b_r.at[s, i], (row, sibling)),
            ))

    def from_sibling(s):
        for i, j in enumerate(theirs):
            copy = remote(xbuf.at[j, s], xbuf.at[j, s], b_s.at[s, i], b_r.at[s, i], (row, sibling))
            guarded(lacks(row), copy.wait_recv)

    def multiply(g, n, way):
        u0, u1 = SPANS[g]
        one, two, n1, n2, index = way["one"], way["two"], way["n1"], way["n2"], way["index"]
        w_at = slice(way["start"] + n * tile, way["start"] + (n + 1) * tile)
        acc = None
        for j in range(ratio):
            term = jnp.dot(
                xbuf[j, u0:u1].reshape((u1 - u0) * nrow * ct, width), w_ref[j * width:(j + 1) * width, w_at],
                preferred_element_type=jnp.float32,
            )
            acc = term if acc is None else acc + term
        acc = acc.reshape(u1 - u0, nrow, ct, tile)
        acc_ref[:u1 - u0] = acc
        low = acc.astype(jnp.bfloat16)
        for i in range(n1):
            for m in range(n2):
                way["p1"][n, i, u0:u1, m] = low[:, index(i, m)]
        for d in range(1, n1):
            to = lax.rem(one + d, n1)
            copy = remote(
                way["p1"].at[n, to, u0:u1], way["r1"].at[n, one, u0:u1],
                way["s1_s"].at[g, n, d - 1], way["s1_r"].at[g, n, one], (index(to, two), col),
            )
            copy.start()
            sends.append((True, copy))
        for m in range(n2):
            way["own1"][n, u0:u1, m] = acc_ref[:u1 - u0, index(one, m)]

    def add_first(g, n, way):
        u0, u1 = SPANS[g]
        one, two, n1, n2, index = way["one"], way["two"], way["n1"], way["n2"], way["index"]
        for d in range(1, n1):
            src = lax.rem(one + d, n1)
            remote(
                way["p1"].at[n, src, u0:u1], way["r1"].at[n, src, u0:u1],
                way["s1_s"].at[g, n, d - 1], way["s1_r"].at[g, n, src], (index(src, two), col),
            ).wait_recv()
        for e in list(range(1, n2)) + [0]:
            to = lax.rem(two + e, n2)
            u = way["own1"][n, u0:u1, to]
            for d in range(1, n1):
                u = u + way["r1"][n, lax.rem(one + d, n1), u0:u1, to].astype(jnp.float32)
            if e:
                way["p2"][n, to, u0:u1] = u.astype(jnp.bfloat16)
                copy = remote(
                    way["p2"].at[n, to, u0:u1], way["r2"].at[n, two, u0:u1],
                    way["s2_s"].at[g, n, e - 1], way["s2_r"].at[g, n, two], (index(one, to), col),
                )
                copy.start()
                sends.append((True, copy))
            else:
                way["own2"][n, u0:u1] = u

    def finish(g, n, way):
        u0, u1 = SPANS[g]
        one, two, n2, index = way["one"], way["two"], way["n2"], way["index"]
        for e in range(1, n2):
            src = lax.rem(two + e, n2)
            remote(
                way["p2"].at[n, src, u0:u1], way["r2"].at[n, src, u0:u1],
                way["s2_s"].at[g, n, e - 1], way["s2_r"].at[g, n, src], (index(one, src), col),
            ).wait_recv()
        u = way["own2"][n, u0:u1]
        for e in range(1, n2):
            u = u + way["r2"][n, lax.rem(two + e, n2), u0:u1].astype(jnp.float32)
        u = 0.5 * u * (1.0 + jnp.tanh(math.sqrt(2.0 / math.pi) * (u + 0.044715 * (u * u * u))))
        w_at = slice(way["start"] + n * tile, way["start"] + (n + 1) * tile)
        out_ref[u0 * ct:u1 * ct, w_at] = u.astype(jnp.bfloat16).reshape((u1 - u0) * ct, tile)

    pieces = [(n, way) for n in range(half // tile) for way in ways]

    def each(fn, g):
        for n, way in pieces:
            fn(g, n, way)

    to_rows(0)
    to_sibling(0)
    last = len(SPANS) - 1
    for g, (u0, u1) in enumerate(SPANS):
        for s in range(u0, u1):
            from_sibling(s)
        if g == 0:
            w_copy.wait()
        if u1 < CHUNKS:
            to_rows(u1)
        each(multiply, g)
        if g < last:
            to_sibling(u1)
            for s in range(u1 + 1, SPANS[g + 1][1]):
                to_rows(s)
                to_sibling(s)
        if g:
            each(add_first, g - 1)
    for g in range(last - 1):
        each(finish, g)
    for i, (n, way) in enumerate(pieces):
        add_first(last, n, way)
        finish(last - 1, n, way)
    each(finish, last)
    for cond, copy in sends:
        guarded(cond, copy.wait_send)


def per_device(q_seq, k_seq, v_seq, resid, ln_gain, w_up):
    nrow, ncol = lax.axis_size("row"), lax.axis_size("col")
    seq, width = q_seq.shape
    depth, cols = w_up.shape
    ratio, nz, ct = ncol // nrow, ncol // CORES, seq // CHUNKS
    per = max(1, ratio // CORES)
    dma = pltpu.SemaphoreType.DMA
    hbm = pl.BlockSpec(memory_space=pltpu.HBM)
    half = cols // 2
    tile = math.gcd(half, TILE)
    nlow = low_count(nrow)
    nhigh = nrow // nlow

    count = half // tile
    span = max(u1 - u0 for u0, u1 in SPANS)

    def sums(n1, n2):
        return [
            pltpu.VMEM((count, n1, CHUNKS, n2, ct, tile), jnp.bfloat16),
            pltpu.VMEM((count, n1, CHUNKS, n2, ct, tile), jnp.bfloat16),
            pltpu.VMEM((count, CHUNKS, n2, ct, tile), jnp.float32),
            pltpu.VMEM((count, n2, CHUNKS, ct, tile), jnp.bfloat16),
            pltpu.VMEM((count, n2, CHUNKS, ct, tile), jnp.bfloat16),
            pltpu.VMEM((count, CHUNKS, ct, tile), jnp.float32),
        ]

    return pl.pallas_call(
        functools.partial(kernel, nrow, ncol),
        out_shape=jax.ShapeDtypeStruct((seq, cols), jnp.bfloat16),
        in_specs=[hbm] * 6,
        out_specs=pl.BlockSpec(memory_space=pltpu.VMEM),
        scratch_shapes=[
            *[pltpu.VMEM((seq, width), jnp.bfloat16)] * 4,
            pltpu.VMEM((1, width), jnp.float32),
            pltpu.VMEM((depth, cols), jnp.bfloat16),
            pltpu.VMEM((seq, width), jnp.float32),
            pltpu.VMEM((ncol, 8, seq), jnp.float32),
            pltpu.VMEM((CHUNKS, nz, ct, width), jnp.bfloat16),
            pltpu.VMEM((ratio, CHUNKS, nrow, ct, width), jnp.bfloat16),
            pltpu.VMEM((span, nrow, ct, tile), jnp.float32),
            *sums(nlow, nhigh),
            *sums(nhigh, nlow),
            dma((5,)),
            dma,
            dma((ncol - 1,)),
            dma((ncol,)),
            dma((CHUNKS, nz - 1)),
            dma((CHUNKS, nz)),
            dma((CHUNKS, per, nrow - 1)),
            dma((CHUNKS, per, nrow)),
            dma((CHUNKS, per)),
            dma((CHUNKS, per)),
            dma((len(SPANS), count, nlow)),
            dma((len(SPANS), count, nlow)),
            dma((len(SPANS), count, nhigh)),
            dma((len(SPANS), count, nhigh)),
            dma((len(SPANS), count, nhigh)),
            dma((len(SPANS), count, nhigh)),
            dma((len(SPANS), count, nlow)),
            dma((len(SPANS), count, nlow)),
        ],
        compiler_params=pltpu.CompilerParams(
            collective_id=0, has_side_effects=True, vmem_limit_bytes=60 * 1024 * 1024
        ),
        cost_estimate=pl.CostEstimate(
            flops=2 * nrow * seq * depth * cols,
            bytes_accessed=2 * (depth * cols + seq * cols + 4 * seq * width),
            transcendentals=seq * cols,
        ),
    )(q_seq, k_seq, v_seq, resid, ln_gain.reshape(1, -1), w_up)


def solution(mesh):
    placed = (
        P("row", "col"),
        P("row", "col"),
        P("row", "col"),
        P("row", "col"),
        P(),
        P("row", "col"),
    )
    return jax.shard_map(
        per_device, mesh=mesh, in_specs=placed, out_specs=P("row", "col"), check_vma=False
    )
```

```python
import functools
import math

import jax
import jax.numpy as jnp
from jax import lax
from jax.experimental import pallas as pl
from jax.experimental.pallas import tpu as pltpu
from jax.sharding import PartitionSpec as P

HD = 128
CORES = 2
CHUNKS = 4
SPANS = ((0, 1), (1, 2), (2, 4))
GROUP = 3
TILE = 512
MESH = pl.DeviceIdType.MESH


def guarded(cond, fn):
    if cond is True:
        fn()
    else:
        pl.when(cond)(fn)


def low_count(nrow):
    return max(n for n in range(1, math.isqrt(nrow) + 1) if nrow % n == 0)


def kernel(
    nrow, ncol,
    q_hbm, k_hbm, v_hbm, resid_hbm, gain_hbm, w_hbm, out_ref,
    q_ref, k_ref, v_ref, resid_ref, gain_ref, w_ref, stream, stats, zbuf, xbuf, acc_ref,
    one_p, one_r, one_own, two_p, two_r, two_own, other_one_p, other_one_r, other_one_own,
    other_two_p, other_two_r, other_two_own,
    in_sem, w_sem, st_s, st_r, z_s, z_r, p_s, p_r, b_s, b_r,
    r1_s, r1_r, r2_s, r2_r, q1_s, q1_r, q2_s, q2_r,
):
    seq, width = q_ref.shape
    cols = out_ref.shape[1]
    half = cols // 2
    tile = math.gcd(half, TILE)
    ratio = ncol // nrow
    nz = ncol // CORES
    ct = seq // CHUNKS
    full = width * ncol
    row, col = lax.axis_index("row"), lax.axis_index("col")
    z, core = lax.div(col, CORES), lax.rem(col, CORES)
    sibling = z * CORES + 1 - core
    sends = []

    def remote(src, dst, send_sem, recv_sem, dev):
        return pltpu.make_async_remote_copy(
            src_ref=src, dst_ref=dst, send_sem=send_sem, recv_sem=recv_sem,
            device_id=dev, device_id_type=MESH,
        )

    loads = [
        pltpu.make_async_copy(src, dst, in_sem.at[i])
        for i, (src, dst) in enumerate((
            (q_hbm, q_ref), (k_hbm, k_ref), (v_hbm, v_ref), (resid_hbm, resid_ref),
            (gain_hbm.at[:, pl.ds(pl.multiple_of(col * width, 128), width)], gain_ref),
        ))
    ]
    w_copy = pltpu.make_async_copy(w_hbm, w_ref, w_sem)
    for load in loads:
        load.start()

    barrier = pltpu.get_barrier_semaphore()
    for d in range(1, ncol):
        pl.semaphore_signal(barrier, inc=1, device_id=(row, lax.rem(col + d, ncol)), device_id_type=MESH)
    for d in range(1, nrow):
        pl.semaphore_signal(barrier, inc=1, device_id=(lax.rem(row + d, nrow), col), device_id_type=MESH)

    for load in loads:
        load.wait()
    w_copy.start()

    causal = lax.broadcasted_iota(jnp.int32, (seq, seq), 0) >= lax.broadcasted_iota(jnp.int32, (seq, seq), 1)
    sum1 = jnp.zeros((seq, HD), jnp.float32)
    sum2 = jnp.zeros((seq, HD), jnp.float32)
    heads = width // HD
    for first in range(0, heads, GROUP):
        cuts = [slice(h * HD, (h + 1) * HD) for h in range(first, min(first + GROUP, heads))]
        scores = [
            lax.dot_general(
                q_ref[:, cut], k_ref[:, cut], (((1,), (1,)), ((), ())), preferred_element_type=jnp.float32
            ) * (1.0 / math.sqrt(HD))
            for cut in cuts
        ]
        scores = [jnp.where(causal, x, -1e30) for x in scores]
        highest = [jnp.max(x, axis=-1, keepdims=True) for x in scores]
        expo = [jnp.exp(x - m) for x, m in zip(scores, highest)]
        below = [jnp.sum(x, axis=-1, keepdims=True) for x in expo]
        prob = [(x / m).astype(jnp.bfloat16) for x, m in zip(expo, below)]
        attended = [
            jnp.dot(x, v_ref[:, cut], preferred_element_type=jnp.float32).astype(jnp.bfloat16)
            for x, cut in zip(prob, cuts)
        ]
        for x, cut in zip(attended, cuts):
            part = resid_ref[:, cut].astype(jnp.float32) + x.astype(jnp.float32)
            stream[:, cut] = part
            sum1 += part
            sum2 += part * part

    place = lax.broadcasted_iota(jnp.int32, (8, seq), 0)
    stats[col] = jnp.where(
        place == 0,
        jnp.sum(sum1.T, axis=0, keepdims=True),
        jnp.where(place == 1, jnp.sum(sum2.T, axis=0, keepdims=True), 0.0),
    )
    pl.semaphore_wait(barrier, ncol + nrow - 2)
    for d in range(1, ncol):
        copy = remote(stats.at[col], stats.at[col], st_s.at[d - 1], st_r.at[col], (row, lax.rem(col + d, ncol)))
        copy.start()
        sends.append((True, copy))
    for d in range(1, ncol):
        other = lax.rem(col + d, ncol)
        remote(stats.at[other], stats.at[other], st_s.at[d - 1], st_r.at[other], (row, other)).wait_recv()
    total = stats[0]
    for c in range(1, ncol):
        total += stats[c]
    spread_out = jnp.concatenate([total] * (seq // 8), axis=0).T
    mean = spread_out[:, 0:1] / full
    spread = spread_out[:, 1:2] / full - mean * mean
    inv = lax.rsqrt(spread + 1e-05)
    gain = gain_ref[...]

    def along_z(s):
        for d in range(1, nz):
            dev = (row, lax.rem(z + d, nz) * CORES + core)
            copy = remote(zbuf.at[s, z], zbuf.at[s, z], z_s.at[s, d - 1], z_r.at[s, z], dev)
            copy.start()
            sends.append((True, copy))

    def normalize(s):
        rows = slice(s * ct, (s + 1) * ct)
        zbuf[s, z] = ((stream[rows, :] - mean[rows]) * inv[rows] * gain).astype(jnp.bfloat16)

    for s in range(CHUNKS):
        normalize(s)
        along_z(s)

    if ratio % CORES == 0:
        mine = [CORES * i + core for i in range(ratio // CORES)]
        theirs = [CORES * i + 1 - core for i in range(ratio // CORES)]
        holds = lambda r: True
        lacks = lambda r: True
    else:
        mine, theirs = [0], [0]
        holds = lambda r: lax.rem(r, CORES) == core
        lacks = lambda r: lax.rem(r, CORES) != core

    nlow = low_count(nrow)
    nhigh = nrow // nlow
    high, low_at = lax.div(row, nlow), lax.rem(row, nlow)
    ways = [
        dict(
            start=0, n1=nlow, n2=nhigh, one=low_at, two=high, index=lambda i, m: m * nlow + i,
            p1=one_p, r1=one_r, own1=one_own, p2=two_p, r2=two_r, own2=two_own,
            s1_s=r1_s, s1_r=r1_r, s2_s=r2_s, s2_r=r2_r,
        ),
        dict(
            start=half, n1=nhigh, n2=nlow, one=high, two=low_at, index=lambda i, m: i * nlow + m,
            p1=other_one_p, r1=other_one_r, own1=other_one_own, p2=other_two_p, r2=other_two_r,
            own2=other_two_own, s1_s=q1_s, s1_r=q1_r, s2_s=q2_s, s2_r=q2_r,
        ),
    ]

    def to_rows(s):
        for d in range(1, nz):
            other = lax.rem(z + d, nz)
            remote(
                zbuf.at[s, other], zbuf.at[s, other], z_s.at[s, d - 1], z_r.at[s, other],
                (row, other * CORES + core),
            ).wait_recv()
        for i, j in enumerate(mine):
            for d in range(1, nrow):
                to = lax.rem(row + d, nrow)
                copy = remote(
                    zbuf.at[s, lax.div(to * ratio + j, CORES)], xbuf.at[j, s, row],
                    p_s.at[s, i, d - 1], p_r.at[s, i, row], (to, col),
                )
                guarded(holds(to), copy.start)
                sends.append((holds(to), copy))

            def keep(j=j):
                xbuf[j, s, row] = zbuf[s, lax.div(row * ratio + j, CORES)]

            guarded(holds(row), keep)

    def to_sibling(s):
        for i, j in enumerate(mine):

            def pass_on(i=i, j=j):
                for d in range(1, nrow):
                    src = lax.rem(row + d, nrow)
                    remote(
                        xbuf.at[j, s, src], xbuf.at[j, s, src], p_s.at[s, i, d - 1], p_r.at[s, i, src],
                        (src, col),
                    ).wait_recv()
                remote(xbuf.at[j, s], xbuf.at[j, s], b_s.at[s, i], b_r.at[s, i], (row, sibling)).start()

            guarded(holds(row), pass_on)
            sends.append((
                holds(row),
                remote(xbuf.at[j, s], xbuf.at[j, s], b_s.at[s, i], b_r.at[s, i], (row, sibling)),
            ))

    def from_sibling(s):
        for i, j in enumerate(theirs):
            copy = remote(xbuf.at[j, s], xbuf.at[j, s], b_s.at[s, i], b_r.at[s, i], (row, sibling))
            guarded(lacks(row), copy.wait_recv)

    def multiply(g, n, way):
        u0, u1 = SPANS[g]
        one, two, n1, n2, index = way["one"], way["two"], way["n1"], way["n2"], way["index"]
        w_at = slice(way["start"] + n * tile, way["start"] + (n + 1) * tile)
        acc = None
        for j in range(ratio):
            term = jnp.dot(
                xbuf[j, u0:u1].reshape((u1 - u0) * nrow * ct, width), w_ref[j * width:(j + 1) * width, w_at],
                preferred_element_type=jnp.float32,
            )
            acc = term if acc is None else acc + term
        acc = acc.reshape(u1 - u0, nrow, ct, tile)
        acc_ref[:u1 - u0] = acc
        low = acc.astype(jnp.bfloat16)
        for i in range(n1):
            for m in range(n2):
                way["p1"][n, i, u0:u1, m] = low[:, index(i, m)]
        for d in range(1, n1):
            to = lax.rem(one + d, n1)
            copy = remote(
                way["p1"].at[n, to, u0:u1], way["r1"].at[n, one, u0:u1],
                way["s1_s"].at[g, n, d - 1], way["s1_r"].at[g, n, one], (index(to, two), col),
            )
            copy.start()
            sends.append((True, copy))
        for m in range(n2):
            way["own1"][n, u0:u1, m] = acc_ref[:u1 - u0, index(one, m)]

    def add_first(g, n, way):
        u0, u1 = SPANS[g]
        one, two, n1, n2, index = way["one"], way["two"], way["n1"], way["n2"], way["index"]
        for d in range(1, n1):
            src = lax.rem(one + d, n1)
            remote(
                way["p1"].at[n, src, u0:u1], way["r1"].at[n, src, u0:u1],
                way["s1_s"].at[g, n, d - 1], way["s1_r"].at[g, n, src], (index(src, two), col),
            ).wait_recv()
        for e in list(range(1, n2)) + [0]:
            to = lax.rem(two + e, n2)
            u = way["own1"][n, u0:u1, to]
            for d in range(1, n1):
                u = u + way["r1"][n, lax.rem(one + d, n1), u0:u1, to].astype(jnp.float32)
            if e:
                way["p2"][n, to, u0:u1] = u.astype(jnp.bfloat16)
                copy = remote(
                    way["p2"].at[n, to, u0:u1], way["r2"].at[n, two, u0:u1],
                    way["s2_s"].at[g, n, e - 1], way["s2_r"].at[g, n, two], (index(one, to), col),
                )
                copy.start()
                sends.append((True, copy))
            else:
                way["own2"][n, u0:u1] = u

    def finish(g, n, way):
        u0, u1 = SPANS[g]
        one, two, n2, index = way["one"], way["two"], way["n2"], way["index"]
        for e in range(1, n2):
            src = lax.rem(two + e, n2)
            remote(
                way["p2"].at[n, src, u0:u1], way["r2"].at[n, src, u0:u1],
                way["s2_s"].at[g, n, e - 1], way["s2_r"].at[g, n, src], (index(one, src), col),
            ).wait_recv()
        u = way["own2"][n, u0:u1]
        for e in range(1, n2):
            u = u + way["r2"][n, lax.rem(two + e, n2), u0:u1].astype(jnp.float32)
        u = 0.5 * u * (1.0 + jnp.tanh(math.sqrt(2.0 / math.pi) * (u + 0.044715 * (u * u * u))))
        w_at = slice(way["start"] + n * tile, way["start"] + (n + 1) * tile)
        out_ref[u0 * ct:u1 * ct, w_at] = u.astype(jnp.bfloat16).reshape((u1 - u0) * ct, tile)

    pieces = [(n, way) for n in range(half // tile) for way in ways]

    def each(fn, g):
        for n, way in pieces:
            fn(g, n, way)

    to_rows(0)
    to_sibling(0)
    last = len(SPANS) - 1
    ahead = 1
    for g, (u0, u1) in enumerate(SPANS):
        if ahead < CHUNKS:
            to_rows(ahead)
            ahead += 1
        if g > 1:
            each(add_first, g - 2)
        for s in range(max(u0, 1), u1):
            to_sibling(s)
            if s + 1 == u1 - 1 and g == last and g > 0:
                each(add_first, g - 1)
        if g == last and g > 0 and u1 - u0 == 1:
            each(add_first, g - 1)
        for s in range(u0, u1):
            from_sibling(s)
        if g == 0:
            w_copy.wait()
        each(multiply, g)
    for g in range(last):
        each(finish, g)
    for n, way in pieces:
        add_first(last, n, way)
    each(finish, last)
    for cond, copy in sends:
        guarded(cond, copy.wait_send)


def per_device(q_seq, k_seq, v_seq, resid, ln_gain, w_up):
    nrow, ncol = lax.axis_size("row"), lax.axis_size("col")
    seq, width = q_seq.shape
    depth, cols = w_up.shape
    ratio, nz, ct = ncol // nrow, ncol // CORES, seq // CHUNKS
    per = max(1, ratio // CORES)
    dma = pltpu.SemaphoreType.DMA
    hbm = pl.BlockSpec(memory_space=pltpu.HBM)
    half = cols // 2
    tile = math.gcd(half, TILE)
    nlow = low_count(nrow)
    nhigh = nrow // nlow

    count = half // tile
    span = max(u1 - u0 for u0, u1 in SPANS)

    def sums(n1, n2):
        return [
            pltpu.VMEM((count, n1, CHUNKS, n2, ct, tile), jnp.bfloat16),
            pltpu.VMEM((count, n1, CHUNKS, n2, ct, tile), jnp.bfloat16),
            pltpu.VMEM((count, CHUNKS, n2, ct, tile), jnp.float32),
            pltpu.VMEM((count, n2, CHUNKS, ct, tile), jnp.bfloat16),
            pltpu.VMEM((count, n2, CHUNKS, ct, tile), jnp.bfloat16),
            pltpu.VMEM((count, CHUNKS, ct, tile), jnp.float32),
        ]

    return pl.pallas_call(
        functools.partial(kernel, nrow, ncol),
        out_shape=jax.ShapeDtypeStruct((seq, cols), jnp.bfloat16),
        in_specs=[hbm] * 6,
        out_specs=pl.BlockSpec(memory_space=pltpu.VMEM),
        scratch_shapes=[
            *[pltpu.VMEM((seq, width), jnp.bfloat16)] * 4,
            pltpu.VMEM((1, width), jnp.float32),
            pltpu.VMEM((depth, cols), jnp.bfloat16),
            pltpu.VMEM((seq, width), jnp.float32),
            pltpu.VMEM((ncol, 8, seq), jnp.float32),
            pltpu.VMEM((CHUNKS, nz, ct, width), jnp.bfloat16),
            pltpu.VMEM((ratio, CHUNKS, nrow, ct, width), jnp.bfloat16),
            pltpu.VMEM((span, nrow, ct, tile), jnp.float32),
            *sums(nlow, nhigh),
            *sums(nhigh, nlow),
            dma((5,)),
            dma,
            dma((ncol - 1,)),
            dma((ncol,)),
            dma((CHUNKS, nz - 1)),
            dma((CHUNKS, nz)),
            dma((CHUNKS, per, nrow - 1)),
            dma((CHUNKS, per, nrow)),
            dma((CHUNKS, per)),
            dma((CHUNKS, per)),
            dma((len(SPANS), count, nlow)),
            dma((len(SPANS), count, nlow)),
            dma((len(SPANS), count, nhigh)),
            dma((len(SPANS), count, nhigh)),
            dma((len(SPANS), count, nhigh)),
            dma((len(SPANS), count, nhigh)),
            dma((len(SPANS), count, nlow)),
            dma((len(SPANS), count, nlow)),
        ],
        compiler_params=pltpu.CompilerParams(
            collective_id=0, has_side_effects=True, vmem_limit_bytes=60 * 1024 * 1024
        ),
        cost_estimate=pl.CostEstimate(
            flops=2 * nrow * seq * depth * cols,
            bytes_accessed=2 * (depth * cols + seq * cols + 4 * seq * width),
            transcendentals=seq * cols,
        ),
    )(q_seq, k_seq, v_seq, resid, ln_gain.reshape(1, -1), w_up)


def solution(mesh):
    placed = (
        P("row", "col"),
        P("row", "col"),
        P("row", "col"),
        P("row", "col"),
        P(),
        P("row", "col"),
    )
    return jax.shard_map(
        per_device, mesh=mesh, in_specs=placed, out_specs=P("row", "col"), check_vma=False
    )
```

```python
import functools
import math

import jax
import jax.numpy as jnp
from jax import lax
from jax.experimental import pallas as pl
from jax.experimental.pallas import tpu as pltpu
from jax.sharding import PartitionSpec as P

HD = 128
CORES = 2
CHUNKS = 4
SPANS = ((0, 1), (1, 2), (2, 3), (3, 4))
GROUP = 3
TILE = 512
MESH = pl.DeviceIdType.MESH


def guarded(cond, fn):
    if cond is True:
        fn()
    else:
        pl.when(cond)(fn)


def low_count(nrow):
    return max(n for n in range(1, math.isqrt(nrow) + 1) if nrow % n == 0)


def kernel(
    nrow, ncol,
    q_hbm, k_hbm, v_hbm, resid_hbm, gain_hbm, w_hbm, out_ref,
    q_ref, k_ref, v_ref, resid_ref, gain_ref, w_ref, stream, stats, zbuf, xbuf, acc_ref,
    one_p, one_r, one_own, two_p, two_r, two_own, other_one_p, other_one_r, other_one_own,
    other_two_p, other_two_r, other_two_own,
    in_sem, w_sem, st_s, st_r, z_s, z_r, p_s, p_r, b_s, b_r,
    r1_s, r1_r, r2_s, r2_r, q1_s, q1_r, q2_s, q2_r,
):
    seq, width = q_ref.shape
    cols = out_ref.shape[1]
    half = cols // 2
    tile = math.gcd(half, TILE)
    ratio = ncol // nrow
    nz = ncol // CORES
    ct = seq // CHUNKS
    full = width * ncol
    row, col = lax.axis_index("row"), lax.axis_index("col")
    z, core = lax.div(col, CORES), lax.rem(col, CORES)
    sibling = z * CORES + 1 - core
    sends = []

    def remote(src, dst, send_sem, recv_sem, dev):
        return pltpu.make_async_remote_copy(
            src_ref=src, dst_ref=dst, send_sem=send_sem, recv_sem=recv_sem,
            device_id=dev, device_id_type=MESH,
        )

    loads = [
        pltpu.make_async_copy(src, dst, in_sem.at[i])
        for i, (src, dst) in enumerate((
            (q_hbm, q_ref), (k_hbm, k_ref), (v_hbm, v_ref), (resid_hbm, resid_ref),
            (gain_hbm.at[:, pl.ds(pl.multiple_of(col * width, 128), width)], gain_ref),
        ))
    ]
    w_copy = pltpu.make_async_copy(w_hbm, w_ref, w_sem)
    for load in loads:
        load.start()

    barrier = pltpu.get_barrier_semaphore()
    for d in range(1, ncol):
        pl.semaphore_signal(barrier, inc=1, device_id=(row, lax.rem(col + d, ncol)), device_id_type=MESH)
    for d in range(1, nrow):
        pl.semaphore_signal(barrier, inc=1, device_id=(lax.rem(row + d, nrow), col), device_id_type=MESH)

    for load in loads:
        load.wait()
    w_copy.start()

    causal = lax.broadcasted_iota(jnp.int32, (seq, seq), 0) >= lax.broadcasted_iota(jnp.int32, (seq, seq), 1)
    sum1 = jnp.zeros((seq, HD), jnp.float32)
    sum2 = jnp.zeros((seq, HD), jnp.float32)
    heads = width // HD
    for first in range(0, heads, GROUP):
        cuts = [slice(h * HD, (h + 1) * HD) for h in range(first, min(first + GROUP, heads))]
        scores = [
            lax.dot_general(
                q_ref[:, cut], k_ref[:, cut], (((1,), (1,)), ((), ())), preferred_element_type=jnp.float32
            ) * (1.0 / math.sqrt(HD))
            for cut in cuts
        ]
        scores = [jnp.where(causal, x, -1e30) for x in scores]
        highest = [jnp.max(x, axis=-1, keepdims=True) for x in scores]
        expo = [jnp.exp(x - m) for x, m in zip(scores, highest)]
        below = [jnp.sum(x, axis=-1, keepdims=True) for x in expo]
        prob = [(x / m).astype(jnp.bfloat16) for x, m in zip(expo, below)]
        attended = [
            jnp.dot(x, v_ref[:, cut], preferred_element_type=jnp.float32).astype(jnp.bfloat16)
            for x, cut in zip(prob, cuts)
        ]
        for x, cut in zip(attended, cuts):
            part = resid_ref[:, cut].astype(jnp.float32) + x.astype(jnp.float32)
            stream[:, cut] = part
            sum1 += part
            sum2 += part * part

    place = lax.broadcasted_iota(jnp.int32, (8, seq), 0)
    stats[col] = jnp.where(
        place == 0,
        jnp.sum(sum1.T, axis=0, keepdims=True),
        jnp.where(place == 1, jnp.sum(sum2.T, axis=0, keepdims=True), 0.0),
    )
    pl.semaphore_wait(barrier, ncol + nrow - 2)
    for d in range(1, ncol):
        copy = remote(stats.at[col], stats.at[col], st_s.at[d - 1], st_r.at[col], (row, lax.rem(col + d, ncol)))
        copy.start()
        sends.append((True, copy))
    for d in range(1, ncol):
        other = lax.rem(col + d, ncol)
        remote(stats.at[other], stats.at[other], st_s.at[d - 1], st_r.at[other], (row, other)).wait_recv()
    total = stats[0]
    for c in range(1, ncol):
        total += stats[c]
    spread_out = jnp.concatenate([total] * (seq // 8), axis=0).T
    mean = spread_out[:, 0:1] / full
    spread = spread_out[:, 1:2] / full - mean * mean
    inv = lax.rsqrt(spread + 1e-05)
    gain = gain_ref[...]

    def along_z(s):
        for d in range(1, nz):
            dev = (row, lax.rem(z + d, nz) * CORES + core)
            copy = remote(zbuf.at[s, z], zbuf.at[s, z], z_s.at[s, d - 1], z_r.at[s, z], dev)
            copy.start()
            sends.append((True, copy))

    def normalize(s):
        rows = slice(s * ct, (s + 1) * ct)
        zbuf[s, z] = ((stream[rows, :] - mean[rows]) * inv[rows] * gain).astype(jnp.bfloat16)

    for s in range(CHUNKS):
        normalize(s)
        along_z(s)

    if ratio % CORES == 0:
        mine = [CORES * i + core for i in range(ratio // CORES)]
        theirs = [CORES * i + 1 - core for i in range(ratio // CORES)]
        holds = lambda r: True
        lacks = lambda r: True
    else:
        mine, theirs = [0], [0]
        holds = lambda r: lax.rem(r, CORES) == core
        lacks = lambda r: lax.rem(r, CORES) != core

    nlow = low_count(nrow)
    nhigh = nrow // nlow
    high, low_at = lax.div(row, nlow), lax.rem(row, nlow)
    ways = [
        dict(
            start=0, n1=nlow, n2=nhigh, one=low_at, two=high, index=lambda i, m: m * nlow + i,
            p1=one_p, r1=one_r, own1=one_own, p2=two_p, r2=two_r, own2=two_own,
            s1_s=r1_s, s1_r=r1_r, s2_s=r2_s, s2_r=r2_r,
        ),
        dict(
            start=half, n1=nhigh, n2=nlow, one=high, two=low_at, index=lambda i, m: i * nlow + m,
            p1=other_one_p, r1=other_one_r, own1=other_one_own, p2=other_two_p, r2=other_two_r,
            own2=other_two_own, s1_s=q1_s, s1_r=q1_r, s2_s=q2_s, s2_r=q2_r,
        ),
    ]

    def to_rows(s):
        for d in range(1, nz):
            other = lax.rem(z + d, nz)
            remote(
                zbuf.at[s, other], zbuf.at[s, other], z_s.at[s, d - 1], z_r.at[s, other],
                (row, other * CORES + core),
            ).wait_recv()
        for i, j in enumerate(mine):
            for d in range(1, nrow):
                to = lax.rem(row + d, nrow)
                copy = remote(
                    zbuf.at[s, lax.div(to * ratio + j, CORES)], xbuf.at[j, s, row],
                    p_s.at[s, i, d - 1], p_r.at[s, i, row], (to, col),
                )
                guarded(holds(to), copy.start)
                sends.append((holds(to), copy))

            def keep(j=j):
                xbuf[j, s, row] = zbuf[s, lax.div(row * ratio + j, CORES)]

            guarded(holds(row), keep)

    def to_sibling(s):
        for i, j in enumerate(mine):

            def pass_on(i=i, j=j):
                for d in range(1, nrow):
                    src = lax.rem(row + d, nrow)
                    remote(
                        xbuf.at[j, s, src], xbuf.at[j, s, src], p_s.at[s, i, d - 1], p_r.at[s, i, src],
                        (src, col),
                    ).wait_recv()
                remote(xbuf.at[j, s], xbuf.at[j, s], b_s.at[s, i], b_r.at[s, i], (row, sibling)).start()

            guarded(holds(row), pass_on)
            sends.append((
                holds(row),
                remote(xbuf.at[j, s], xbuf.at[j, s], b_s.at[s, i], b_r.at[s, i], (row, sibling)),
            ))

    def from_sibling(s):
        for i, j in enumerate(theirs):
            copy = remote(xbuf.at[j, s], xbuf.at[j, s], b_s.at[s, i], b_r.at[s, i], (row, sibling))
            guarded(lacks(row), copy.wait_recv)

    def multiply(g, n, way):
        u0, u1 = SPANS[g]
        one, two, n1, n2, index = way["one"], way["two"], way["n1"], way["n2"], way["index"]
        w_at = slice(way["start"] + n * tile, way["start"] + (n + 1) * tile)
        acc = None
        for j in range(ratio):
            term = jnp.dot(
                xbuf[j, u0:u1].reshape((u1 - u0) * nrow * ct, width), w_ref[j * width:(j + 1) * width, w_at],
                preferred_element_type=jnp.float32,
            )
            acc = term if acc is None else acc + term
        acc = acc.reshape(u1 - u0, nrow, ct, tile)
        acc_ref[:u1 - u0] = acc
        low = acc.astype(jnp.bfloat16)
        for i in range(n1):
            for m in range(n2):
                way["p1"][n, i, u0:u1, m] = low[:, index(i, m)]
        for d in range(1, n1):
            to = lax.rem(one + d, n1)
            copy = remote(
                way["p1"].at[n, to, u0:u1], way["r1"].at[n, one, u0:u1],
                way["s1_s"].at[g, n, d - 1], way["s1_r"].at[g, n, one], (index(to, two), col),
            )
            copy.start()
            sends.append((True, copy))
        for m in range(n2):
            way["own1"][n, u0:u1, m] = acc_ref[:u1 - u0, index(one, m)]

    def add_first(g, n, way):
        u0, u1 = SPANS[g]
        one, two, n1, n2, index = way["one"], way["two"], way["n1"], way["n2"], way["index"]
        for d in range(1, n1):
            src = lax.rem(one + d, n1)
            remote(
                way["p1"].at[n, src, u0:u1], way["r1"].at[n, src, u0:u1],
                way["s1_s"].at[g, n, d - 1], way["s1_r"].at[g, n, src], (index(src, two), col),
            ).wait_recv()
        for e in list(range(1, n2)) + [0]:
            to = lax.rem(two + e, n2)
            u = way["own1"][n, u0:u1, to]
            for d in range(1, n1):
                u = u + way["r1"][n, lax.rem(one + d, n1), u0:u1, to].astype(jnp.float32)
            if e:
                way["p2"][n, to, u0:u1] = u.astype(jnp.bfloat16)
                copy = remote(
                    way["p2"].at[n, to, u0:u1], way["r2"].at[n, two, u0:u1],
                    way["s2_s"].at[g, n, e - 1], way["s2_r"].at[g, n, two], (index(one, to), col),
                )
                copy.start()
                sends.append((True, copy))
            else:
                way["own2"][n, u0:u1] = u

    def finish(g, n, way):
        u0, u1 = SPANS[g]
        one, two, n2, index = way["one"], way["two"], way["n2"], way["index"]
        for e in range(1, n2):
            src = lax.rem(two + e, n2)
            remote(
                way["p2"].at[n, src, u0:u1], way["r2"].at[n, src, u0:u1],
                way["s2_s"].at[g, n, e - 1], way["s2_r"].at[g, n, src], (index(one, src), col),
            ).wait_recv()
        u = way["own2"][n, u0:u1]
        for e in range(1, n2):
            u = u + way["r2"][n, lax.rem(two + e, n2), u0:u1].astype(jnp.float32)
        u = 0.5 * u * (1.0 + jnp.tanh(math.sqrt(2.0 / math.pi) * (u + 0.044715 * (u * u * u))))
        w_at = slice(way["start"] + n * tile, way["start"] + (n + 1) * tile)
        out_ref[u0 * ct:u1 * ct, w_at] = u.astype(jnp.bfloat16).reshape((u1 - u0) * ct, tile)

    pieces = [(n, way) for n in range(half // tile) for way in ways]

    def each(fn, g):
        for n, way in pieces:
            fn(g, n, way)

    to_rows(0)
    to_sibling(0)
    last = len(SPANS) - 1
    ahead = 1
    for g, (u0, u1) in enumerate(SPANS):
        if ahead < CHUNKS:
            to_rows(ahead)
            ahead += 1
        if g > 1:
            each(add_first, g - 2)
        for s in range(max(u0, 1), u1):
            to_sibling(s)
            if s + 1 == u1 - 1 and g == last and g > 0:
                each(add_first, g - 1)
        if g == last and g > 0 and u1 - u0 == 1:
            each(add_first, g - 1)
        for s in range(u0, u1):
            from_sibling(s)
        if g == 0:
            w_copy.wait()
        each(multiply, g)
    for g in range(last):
        each(finish, g)
    for n, way in pieces:
        add_first(last, n, way)
    each(finish, last)
    for cond, copy in sends:
        guarded(cond, copy.wait_send)


def per_device(q_seq, k_seq, v_seq, resid, ln_gain, w_up):
    nrow, ncol = lax.axis_size("row"), lax.axis_size("col")
    seq, width = q_seq.shape
    depth, cols = w_up.shape
    ratio, nz, ct = ncol // nrow, ncol // CORES, seq // CHUNKS
    per = max(1, ratio // CORES)
    dma = pltpu.SemaphoreType.DMA
    hbm = pl.BlockSpec(memory_space=pltpu.HBM)
    half = cols // 2
    tile = math.gcd(half, TILE)
    nlow = low_count(nrow)
    nhigh = nrow // nlow

    count = half // tile
    span = max(u1 - u0 for u0, u1 in SPANS)

    def sums(n1, n2):
        return [
            pltpu.VMEM((count, n1, CHUNKS, n2, ct, tile), jnp.bfloat16),
            pltpu.VMEM((count, n1, CHUNKS, n2, ct, tile), jnp.bfloat16),
            pltpu.VMEM((count, CHUNKS, n2, ct, tile), jnp.float32),
            pltpu.VMEM((count, n2, CHUNKS, ct, tile), jnp.bfloat16),
            pltpu.VMEM((count, n2, CHUNKS, ct, tile), jnp.bfloat16),
            pltpu.VMEM((count, CHUNKS, ct, tile), jnp.float32),
        ]

    return pl.pallas_call(
        functools.partial(kernel, nrow, ncol),
        out_shape=jax.ShapeDtypeStruct((seq, cols), jnp.bfloat16),
        in_specs=[hbm] * 6,
        out_specs=pl.BlockSpec(memory_space=pltpu.VMEM),
        scratch_shapes=[
            *[pltpu.VMEM((seq, width), jnp.bfloat16)] * 4,
            pltpu.VMEM((1, width), jnp.float32),
            pltpu.VMEM((depth, cols), jnp.bfloat16),
            pltpu.VMEM((seq, width), jnp.float32),
            pltpu.VMEM((ncol, 8, seq), jnp.float32),
            pltpu.VMEM((CHUNKS, nz, ct, width), jnp.bfloat16),
            pltpu.VMEM((ratio, CHUNKS, nrow, ct, width), jnp.bfloat16),
            pltpu.VMEM((span, nrow, ct, tile), jnp.float32),
            *sums(nlow, nhigh),
            *sums(nhigh, nlow),
            dma((5,)),
            dma,
            dma((ncol - 1,)),
            dma((ncol,)),
            dma((CHUNKS, nz - 1)),
            dma((CHUNKS, nz)),
            dma((CHUNKS, per, nrow - 1)),
            dma((CHUNKS, per, nrow)),
            dma((CHUNKS, per)),
            dma((CHUNKS, per)),
            dma((len(SPANS), count, nlow)),
            dma((len(SPANS), count, nlow)),
            dma((len(SPANS), count, nhigh)),
            dma((len(SPANS), count, nhigh)),
            dma((len(SPANS), count, nhigh)),
            dma((len(SPANS), count, nhigh)),
            dma((len(SPANS), count, nlow)),
            dma((len(SPANS), count, nlow)),
        ],
        compiler_params=pltpu.CompilerParams(
            collective_id=0, has_side_effects=True, vmem_limit_bytes=60 * 1024 * 1024
        ),
        cost_estimate=pl.CostEstimate(
            flops=2 * nrow * seq * depth * cols,
            bytes_accessed=2 * (depth * cols + seq * cols + 4 * seq * width),
            transcendentals=seq * cols,
        ),
    )(q_seq, k_seq, v_seq, resid, ln_gain.reshape(1, -1), w_up)


def solution(mesh):
    placed = (
        P("row", "col"),
        P("row", "col"),
        P("row", "col"),
        P("row", "col"),
        P(),
        P("row", "col"),
    )
    return jax.shard_map(
        per_device, mesh=mesh, in_specs=placed, out_specs=P("row", "col"), check_vma=False
    )
```
